256 devices in a mesh: ctx: 32 (over y, z_hi, x), head: 8 (over z_lo, core).
Axes of the slice: x: 4, y: 4, z: 8 (z_hi: 2, z_lo: 4; z = z_hi * 4 + z_lo), core: 2. Of those that a mesh axis runs over, the one named last changes fastest.
Arguments:
- window_input: bfloat16 [32, 2048, 768], P('head', 'ctx'), may hold values from -256 to 256
- norm_gain: float32 [768], replicated, may hold values from 0.25 to 1.75
- w_query: bfloat16 [768, 512], replicated, may hold values from -1 to 1
- w_key: bfloat16 [768, 512], replicated, may hold values from -1 to 1
- w_value: bfloat16 [768, 768], replicated, may hold values from -0.21875 to 0.21875
- w_out: bfloat16 [768, 768], replicated, may hold values from -0.21875 to 0.21875
- conv_weight: bfloat16 [2, 3, 768, 384], replicated, may hold values from -0.125 to 0.125
- point_weight: bfloat16 [2, 384, 768], replicated, may hold values from -0.3125 to 0.3125
- dilations: int32 [2], replicated, may hold values from 1 to 16, as said below
- tangent_query: bfloat16 [768, 512], replicated, may hold values from -0.21875 to 0.21875
- tangent_key: bfloat16 [768, 512], replicated, may hold values from -0.21875 to 0.21875
- curvature: float32 [32, 2048], P('head', 'ctx'), may hold values from 0.25 to 4
Outputs:
- output_tangent: bfloat16 [32, 2048, 768], P('head', 'ctx')
- input_cotangent: bfloat16 [32, 2048, 768], P('head', 'ctx')
- gv_query: float32 [768, 512], P(('ctx', 'head'))
- gv_key: float32 [768, 512], P(('ctx', 'head'))
The draws below stay inside these ranges and needn't reach their ends.
Inputs may be any that keep to these rules, and one draw needn't show every extreme that they name: At least one of the two dilations equals 16.
All inputs are finite; a program needn't handle non-finite values.
Results may differ from the reference program's by a relative error of at most 0.015.
The reference program's roundings to bfloat16 on the way (of `normed`, `attended`, `tangent_attended`, `grad_inner`, `grad_attended` and `grad_scores`) count: a program that leaves them out, or rounds other values in their place, can miss the bound.
Values may be sent and summed in bfloat16 or wider, within the bound.
A program may use at most 128 MiB of HBM per device.

```python
import math
import jax
import jax.numpy as jnp
from jax import lax

C = 768
HEADS = 8
KEY = 64
VAL = 96
F = 384
DMAX = 16
L_DEV = 64
B_DEV = 4
L = 2048
SEQS = 32
N_CTX = 32
N_HEAD = 8


def draw_window_input(key, part):
    key = jax.random.fold_in(key, 5)
    key_base, key_rows, key_cols = jax.random.split(key, 3)
    row_scale = jnp.exp(jax.random.uniform(key_rows, (SEQS, L, 1), minval=math.log(0.5), maxval=math.log(5.0)))
    col_scale = jnp.exp(jax.random.uniform(key_cols, (1, 1, C), minval=math.log(0.5), maxval=math.log(5.0)))
    noise = jax.random.normal(key_base, (SEQS, L, C))
    values = noise * row_scale * col_scale
    key_perm = jax.random.fold_in(key, 31)
    key_spike = jax.random.fold_in(key, 32)
    devices_all = N_CTX * N_HEAD
    pairing = jax.random.permutation(key_perm, devices_all)
    owner = (jnp.arange(L) // L_DEV).reshape((1, L)) * N_HEAD + (jnp.arange(SEQS) // B_DEV).reshape((SEQS, 1))
    block_of = jnp.take(pairing, owner)
    feature_block = jnp.arange(C) // (C // devices_all)
    spiked = feature_block.reshape((1, 1, C)) == block_of[..., None]
    spike_values = 24.0 * row_scale * jax.random.normal(key_spike, (SEQS, L, C))
    values = jnp.where(spiked, spike_values, values)
    return jnp.clip(values, -256.0, 256.0).astype(jnp.bfloat16)


def draw_w_query(key, part):
    key = jax.random.fold_in(key, 7)
    matrix = jax.random.normal(key, (C, HEADS, KEY)) / math.sqrt(C)
    return jnp.clip(matrix, -1.0, 1.0).reshape((C, HEADS * KEY)).astype(jnp.bfloat16)


def draw_w_key(key, part):
    key = jax.random.fold_in(key, 8)
    matrix = jax.random.normal(key, (C, HEADS, KEY)) / math.sqrt(C)
    return jnp.clip(matrix, -1.0, 1.0).reshape((C, HEADS * KEY)).astype(jnp.bfloat16)


def draw_dilations(key, part):
    key = jax.random.fold_in(key, 9)
    key_pick, key_other = jax.random.split(key)
    chosen = jax.random.randint(key_pick, (), 0, 2)
    other = jax.random.randint(key_other, (), 1, DMAX + 1)
    return jnp.where(jnp.arange(2) == chosen, DMAX, other).astype(jnp.int32)


def levels(key, shape, cuts, smallest, high):
    def one(dim, blocks):
        draws = jax.random.uniform(jax.random.fold_in(jax.random.fold_in(key, 6), dim), (blocks,), jnp.float32, smallest / len(cuts), high / len(cuts))
        return jnp.repeat(jnp.exp(draws), shape[dim] // blocks).reshape((-1,) + (1,) * (len(shape) - dim - 1))

    gain = one(*cuts[0])
    for cut in cuts[1:]:
        gain = gain * one(*cut)
    return gain


def normal_values(key, extent, scale, bound, kind=jnp.bfloat16):
    return jnp.clip(scale * jax.random.normal(key, extent, jnp.float32), -bound, bound).astype(kind)


def setup_inputs(seed: int = 0) -> dict:
    streams_of = jax.random.split(jax.random.key(seed), 13)
    window_input = draw_window_input(jax.random.fold_in(streams_of[12], 71), 0)
    norm_gain = jnp.clip(1.0 + 0.15 * jax.random.normal(streams_of[1], (C,), jnp.float32), 0.25, 1.75)
    w_query = draw_w_query(jax.random.fold_in(streams_of[12], 71), 0)
    w_key = draw_w_key(jax.random.fold_in(streams_of[12], 71), 0)
    w_value = normal_values(streams_of[4], (C, HEADS * VAL), C ** -0.5, 0.21875)
    w_out = normal_values(streams_of[5], (HEADS * VAL, C), (HEADS * VAL) ** -0.5, 0.21875)
    conv_weight = normal_values(streams_of[6], (2, 3, C, F), (3 * C) ** -0.5, 0.125)
    point_weight = normal_values(streams_of[7], (2, F, C), F ** -0.5, 0.3125)
    dilations = draw_dilations(jax.random.fold_in(streams_of[12], 71), 0)
    tangent_query = normal_values(streams_of[9], (C, HEADS * KEY), C ** -0.5, 0.21875)
    tangent_key = normal_values(streams_of[10], (C, HEADS * KEY), C ** -0.5, 0.21875)
    curvature = jnp.clip(jnp.exp(math.log(4.0) - 2.7725887 * jax.random.uniform(streams_of[11], (SEQS, L), jnp.float32) ** levels(streams_of[11], (SEQS, L), ((0, 8), (1, 32)), -0.2, 0.2)), 0.25, 4.0)
    return {"window_input": window_input, "norm_gain": norm_gain, "w_query": w_query, "w_key": w_key, "w_value": w_value, "w_out": w_out, "conv_weight": conv_weight, "point_weight": point_weight, "dilations": dilations, "tangent_query": tangent_query, "tangent_key": tangent_key, "curvature": curvature}


def gelu_pair(values):
    return jax.jvp(jax.nn.gelu, (values,), (jnp.ones_like(values),))

def to_items(array, depth):
    return array.reshape(SEQS, L, HEADS, depth).transpose(0, 2, 1, 3).reshape(SEQS * HEADS, L, depth)

def to_rows(array, depth):
    return array.reshape(SEQS, HEADS, L, depth).transpose(0, 2, 1, 3).reshape(SEQS * L, HEADS * depth)

def forward_item(operands):
    queries, key_rows, value_rows, tangent_queries, tangent_keys = operands
    score_scale = KEY ** (-0.5)
    scores = jnp.dot(queries, key_rows.T, preferred_element_type=jnp.float32) * score_scale
    weights = jax.nn.softmax(scores, axis=-1)
    attended = jnp.dot(weights.astype(jnp.bfloat16), value_rows, preferred_element_type=jnp.float32).astype(jnp.bfloat16)
    tangent_scores = (jnp.dot(tangent_queries, key_rows.T, preferred_element_type=jnp.float32) + jnp.dot(queries, tangent_keys.T, preferred_element_type=jnp.float32)) * score_scale
    tangent_weights = weights * (tangent_scores - lax.optimization_barrier(jnp.sum(weights * tangent_scores, axis=-1, keepdims=True)))
    tangent_attended = jnp.dot(tangent_weights.astype(jnp.bfloat16), value_rows, preferred_element_type=jnp.float32).astype(jnp.bfloat16)
    return (attended, tangent_attended)

def backward_item(operands):
    queries, key_rows, value_rows, grad_attended = operands
    score_scale = KEY ** (-0.5)
    scores = jnp.dot(queries, key_rows.T, preferred_element_type=jnp.float32) * score_scale
    weights = jax.nn.softmax(scores, axis=-1)
    grad_weights = jnp.dot(grad_attended, value_rows.T, preferred_element_type=jnp.float32)
    grad_scores = (weights * (grad_weights - lax.optimization_barrier(jnp.sum(weights * grad_weights, axis=-1, keepdims=True))) * score_scale).astype(jnp.bfloat16)
    grad_queries = jnp.dot(grad_scores, key_rows, preferred_element_type=jnp.float32).astype(jnp.bfloat16)
    grad_keys = jnp.dot(grad_scores.T, queries, preferred_element_type=jnp.float32).astype(jnp.bfloat16)
    grad_values = jnp.dot(weights.astype(jnp.bfloat16).T, grad_attended, preferred_element_type=jnp.float32).astype(jnp.bfloat16)
    return (grad_queries, grad_keys, grad_values)

def shifted(padded, offset):
    return lax.dynamic_slice_in_dim(padded, offset.astype(jnp.int32), L, 1)

def padding(array):
    return jnp.pad(array, ((0, 0), (DMAX, DMAX), (0, 0)))

def reference(window_input, norm_gain, w_query, w_key, w_value, w_out, conv_weight, point_weight, dilations, tangent_query, tangent_key, curvature):
    inputs = window_input.astype(jnp.float32).reshape(SEQS * L, C)
    spread = jnp.sqrt(lax.optimization_barrier(jnp.mean(inputs * inputs, axis=-1, keepdims=True)) + 1e-06)
    normed = (inputs / spread * norm_gain).astype(jnp.bfloat16)

    def project(weight, depth):
        return to_items(jnp.dot(normed, weight, preferred_element_type=jnp.float32).astype(jnp.bfloat16), depth)
    queries = project(w_query, KEY)
    key_rows = project(w_key, KEY)
    value_rows = project(w_value, VAL)
    tangent_queries = project(tangent_query, KEY)
    tangent_keys = project(tangent_key, KEY)
    attended, tangent_attended = lax.map(forward_item, (queries, key_rows, value_rows, tangent_queries, tangent_keys))
    mixed = inputs + jnp.dot(to_rows(attended, VAL), w_out, preferred_element_type=jnp.float32)
    tangent_mixed = jnp.dot(to_rows(tangent_attended, VAL), w_out, preferred_element_type=jnp.float32)
    slopes = []
    for layer_index in range(2):
        dilation = dilations[layer_index]
        activated, act_slope = gelu_pair(mixed)
        act_pad = padding(activated.astype(jnp.bfloat16).reshape(SEQS, L, C))
        tangent_pad = padding((act_slope * tangent_mixed).astype(jnp.bfloat16).reshape(SEQS, L, C))
        inner = jnp.zeros((SEQS * L, F), jnp.float32)
        tangent_inner = jnp.zeros((SEQS * L, F), jnp.float32)
        for tap_index in range(3):
            offset = DMAX + (tap_index - 1) * dilation
            kernel = conv_weight[layer_index, tap_index]
            inner = inner + jnp.dot(shifted(act_pad, offset).reshape(SEQS * L, C), kernel, preferred_element_type=jnp.float32)
            tangent_inner = tangent_inner + jnp.dot(shifted(tangent_pad, offset).reshape(SEQS * L, C), kernel, preferred_element_type=jnp.float32)
        hidden_value, hidden_slope = gelu_pair(inner)
        mixed = mixed + jnp.dot(hidden_value.astype(jnp.bfloat16), point_weight[layer_index], preferred_element_type=jnp.float32)
        tangent_mixed = tangent_mixed + jnp.dot((hidden_slope * tangent_inner).astype(jnp.bfloat16), point_weight[layer_index], preferred_element_type=jnp.float32)
        slopes.append((act_slope, hidden_slope, dilation))
    output_tangent = tangent_mixed.astype(jnp.bfloat16).reshape(SEQS, L, C)
    gradient = curvature.reshape(SEQS * L, 1) * tangent_mixed
    for layer_index in (1, 0):
        act_slope, hidden_slope, dilation = slopes[layer_index]
        grad_inner = (jnp.dot(gradient.astype(jnp.bfloat16), point_weight[layer_index].T, preferred_element_type=jnp.float32) * hidden_slope).astype(jnp.bfloat16)
        grad_pad = padding(grad_inner.reshape(SEQS, L, F))
        grad_act = jnp.zeros((SEQS * L, C), jnp.float32)
        for tap_index in range(3):
            offset = DMAX - (tap_index - 1) * dilation
            grad_act = grad_act + jnp.dot(shifted(grad_pad, offset).reshape(SEQS * L, F), conv_weight[layer_index, tap_index].T, preferred_element_type=jnp.float32)
        gradient = gradient + grad_act * act_slope
    grad_attended = to_items(jnp.dot(gradient.astype(jnp.bfloat16), w_out.T, preferred_element_type=jnp.float32).astype(jnp.bfloat16), VAL)
    grad_queries, grad_keys, grad_values = lax.map(backward_item, (queries, key_rows, value_rows, grad_attended))
    grad_queries = to_rows(grad_queries, KEY)
    grad_keys = to_rows(grad_keys, KEY)
    grad_values = to_rows(grad_values, VAL)
    tokens = SEQS * L
    gv_query = jnp.dot(normed.T, grad_queries, preferred_element_type=jnp.float32) / tokens
    gv_key = jnp.dot(normed.T, grad_keys, preferred_element_type=jnp.float32) / tokens
    grad_normed = jnp.dot(grad_queries, w_query.T, preferred_element_type=jnp.float32) + jnp.dot(grad_keys, w_key.T, preferred_element_type=jnp.float32) + jnp.dot(grad_values, w_value.T, preferred_element_type=jnp.float32)
    gained = grad_normed * norm_gain
    input_cotangent = gradient + gained / spread - inputs * lax.optimization_barrier(jnp.sum(gained * inputs, axis=-1, keepdims=True)) / (C * spread * spread * spread)
    return (output_tangent, input_cotangent.astype(jnp.bfloat16).reshape(SEQS, L, C), gv_query, gv_key)
```

```python
import functools

import jax
import jax.numpy as jnp
from jax import lax
from jax.experimental import pallas as pl
from jax.experimental.pallas import tpu as pltpu
from jax.sharding import PartitionSpec as P

HEADS = 8
KEY = 64
VAL = 96
DMAX = 16
MESH = pl.DeviceIdType.MESH
VMEM_LIMIT = 56 * 2**20
F32 = jnp.float32
BF16 = jnp.bfloat16
BLOCK = 256


def place(ctx, head):
    return ctx // 8, (ctx // 4) % 2 * 4 + head // 2, ctx % 4, head % 2


def device(y, z, x, core):
    return y * 8 + z // 4 * 4 + x, z % 4 * 2 + core


def chunk_of(ctx, head):
    y, _, x, core = place(ctx, head)
    return (x + 4 - y) % 4 * 2 + core


def member(ctx, head, j):
    y, z, _, _ = place(ctx, head)
    return device(y, z, (j // 2 + y) % 4, j % 2)


def home_of(ctx, head, b):
    y, z, _, core = place(ctx, head)
    return device(b, core * 4 + (z % 4 + 2) % 4, (y + b) % 4, z // 4)


def owner_of(ctx, head, x0):
    y, z, x, core = place(ctx, head)
    return device((x + 4 - y) % 4, core * 4 + (z % 4 + 2) % 4, x0, z // 4)


def me():
    return lax.axis_index("ctx"), lax.axis_index("head")


def signal(barrier, target):
    pl.semaphore_signal(barrier, inc=1, device_id=target, device_id_type=MESH)


def remote(src, dst, send, recv, target):
    return pltpu.make_async_remote_copy(
        src_ref=src, dst_ref=dst, send_sem=send, recv_sem=recv, device_id=target, device_id_type=MESH
    )


class Stream:
    def __init__(self, count, dst, src, slot, own):
        self.count, self.dst, self.src, self.slot, self.own = count, dst, src, slot, own


def home_stream():
    ctx, head = me()
    return Stream(4, lambda i: home_of(ctx, head, i), lambda k: owner_of(ctx, head, k), ctx % 4, None)


def owner_stream():
    ctx, head = me()
    return Stream(4, lambda i: owner_of(ctx, head, i), lambda k: home_of(ctx, head, k), ctx // 8, None)


def group_stream():
    ctx, head = me()
    return Stream(
        8, lambda i: member(ctx, head, i), lambda k: member(ctx, head, k), chunk_of(ctx, head), chunk_of(ctx, head)
    )


def plane_stream():
    ctx, head = me()
    y, z, _, _ = place(ctx, head)
    j = chunk_of(ctx, head)

    def at(r):
        y_at = (r // 8 + 3) % 4
        return device(y_at, r % 8, (j // 2 + y_at) % 4, j % 2)

    rank = (y + 1) % 4 * 8 + z
    return Stream(32, at, at, rank, rank)


def rows_stream():
    ctx, head = me()
    y, z, _, _ = place(ctx, head)
    r = (y + 1) % 4 * 8 + z

    def src(k):
        row = ctx // 8
        y_src = (row + 3) % 4
        return device(y_src, ctx % 8, (k // 2 + y_src) % 4, k % 2)

    return Stream(8, lambda i: (r, i), src, chunk_of(ctx, head), None)


def exchange(arrays, kinds, collective_id):
    count = len(arrays)

    def kernel(*refs):
        xs, outs, sems = refs[:count], refs[count : 2 * count], refs[2 * count :]
        streams = [kind() for kind in kinds]
        barrier = pltpu.get_barrier_semaphore()
        total = 0
        for stream in streams:
            first = 0 if stream.own is None else 1
            base = 0 if stream.own is None else stream.own

            def greet(i, carry, stream=stream, base=base):
                signal(barrier, stream.src((base + i) % stream.count))
                return carry

            lax.fori_loop(first, stream.count, greet, 0)
            total += stream.count - first
        pl.semaphore_wait(barrier, total)
        for n, stream in enumerate(streams):
            x_ref, o_ref, send, recv = xs[n], outs[n], sems[2 * n], sems[2 * n + 1]
            first = 0 if stream.own is None else 1
            base = stream.slot if stream.own is None else stream.own

            def start(i, carry, stream=stream, base=base, x_ref=x_ref, o_ref=o_ref, send=send, recv=recv):
                k = (base + i) % stream.count
                remote(x_ref.at[k], o_ref.at[stream.slot], send.at[k], recv.at[stream.slot], stream.dst(k)).start()
                return carry

            lax.fori_loop(first, stream.count, start, 0)
            if first:
                local = pltpu.make_async_copy(x_ref.at[base], o_ref.at[base], send.at[base])
                local.start()
                local.wait()
        for n, stream in enumerate(streams):
            x_ref, o_ref, send, recv = xs[n], outs[n], sems[2 * n], sems[2 * n + 1]
            first = 0 if stream.own is None else 1
            base = stream.slot if stream.own is None else stream.own

            def finish(i, carry, stream=stream, base=base, x_ref=x_ref, o_ref=o_ref, send=send, recv=recv):
                k = (base + i) % stream.count
                remote(x_ref.at[k], o_ref.at[k], send.at[k], recv.at[k], stream.dst(k)).wait()
                return carry

            lax.fori_loop(first, stream.count, finish, 0)

    scratch = []
    for array in arrays:
        scratch += [pltpu.SemaphoreType.DMA((array.shape[0],))] * 2
    return pl.pallas_call(
        kernel,
        out_shape=[jax.ShapeDtypeStruct(a.shape, a.dtype) for a in arrays],
        in_specs=[pl.BlockSpec(memory_space=pl.ANY)] * count,
        out_specs=[pl.BlockSpec(memory_space=pl.ANY)] * count,
        scratch_shapes=scratch,
        compiler_params=pltpu.CompilerParams(collective_id=collective_id, has_side_effects=True),
    )(*arrays)


def gather(rows, collective_id):
    def kernel(x_ref, o_ref, send, recv, fsend, frecv, local):
        ctx, head = me()
        j = chunk_of(ctx, head)
        core = j % 2
        sibling = member(ctx, head, j - core + 1 - core)
        barrier = pltpu.get_barrier_semaphore()
        signal(barrier, sibling)
        for d in range(1, 4):
            signal(barrier, member(ctx, head, (j + 2 * d) % 8))
        pl.semaphore_wait(barrier, 4)
        for d in range(1, 4):
            remote(x_ref, o_ref.at[j], send.at[d], recv.at[d], member(ctx, head, (j + 2 * d) % 8)).start()
        remote(x_ref, o_ref.at[j], send.at[0], recv.at[0], sibling).start()
        own = pltpu.make_async_copy(x_ref, o_ref.at[j], local)
        own.start()
        for d in (1, 3, 2):
            s = (j + 8 - 2 * d) % 8
            remote(x_ref, o_ref.at[s], send.at[d], recv.at[d], sibling).wait_recv()
            remote(o_ref.at[s], o_ref.at[s], fsend.at[d], frecv.at[d], sibling).start()
        own.wait()
        other = j - core + 1 - core
        remote(x_ref, o_ref.at[other], send.at[0], recv.at[0], sibling).wait()
        for d in (1, 3, 2):
            s = (other + 8 - 2 * d) % 8
            remote(o_ref.at[s], o_ref.at[s], fsend.at[d], frecv.at[d], sibling).wait()
            remote(x_ref, o_ref.at[s], send.at[d], recv.at[d], sibling).wait_send()

    return pl.pallas_call(
        kernel,
        out_shape=jax.ShapeDtypeStruct((8,) + rows.shape, rows.dtype),
        in_specs=[pl.BlockSpec(memory_space=pl.ANY)],
        out_specs=pl.BlockSpec(memory_space=pl.ANY),
        scratch_shapes=[pltpu.SemaphoreType.DMA((4,))] * 4 + [pltpu.SemaphoreType.DMA],
        compiler_params=pltpu.CompilerParams(collective_id=collective_id, has_side_effects=True),
    )(rows)


def dot(a, b, contract):
    return lax.dot_general(a, b, ((contract[0], contract[1]), ((), ())), preferred_element_type=F32)


def attend_forward_kernel(qt_ref, q_ref, kt_ref, k_ref, v_ref, o_ref, lse_ref, att_ref):
    scale = KEY**-0.5
    s = dot(q_ref[...], k_ref[...], ((1,), (1,))) * scale
    top = jnp.max(s, axis=1, keepdims=True)
    p = jnp.exp(s - top)
    ext = dot(p.astype(BF16), v_ref[...], ((1,), (0,)))
    total = ext[:, VAL : VAL + 1]
    inv = 1.0 / total
    ts = dot(qt_ref[...], kt_ref[...], ((1,), (1,))) * scale
    mean = jnp.sum(p * ts, axis=1, keepdims=True) / jnp.sum(p, axis=1, keepdims=True)
    tw = p * (ts - mean)
    tan = dot(tw.astype(BF16), v_ref[...], ((1,), (0,))) * inv
    att = ext * inv
    o_ref[...] = jnp.concatenate([att[:, :VAL], tan[:, :VAL]], axis=1).astype(BF16)
    att_ref[...] = att
    lse = jnp.broadcast_to(top + jnp.log(total), (BLOCK, 128))
    lse_ref[...] = lse.T[:8]


def attend_forward(proj):
    length = proj.shape[0]
    q, tq = proj[:, :KEY], proj[:, KEY : 2 * KEY]
    k, tk = proj[:, 2 * KEY : 3 * KEY], proj[:, 3 * KEY : 4 * KEY]
    qt = jnp.concatenate([tq, q], axis=1)
    kt = jnp.concatenate([k, tk], axis=1)
    v = jnp.concatenate([proj[:, 4 * KEY :], jnp.ones((length, 128 - VAL), BF16)], axis=1)
    whole = lambda a: pl.BlockSpec(a.shape, lambda i: (0, 0))
    part = lambda a: pl.BlockSpec((BLOCK, a.shape[1]), lambda i: (i, 0))
    out, lse, att = pl.pallas_call(
        attend_forward_kernel,
        grid=(length // BLOCK,),
        out_shape=[
            jax.ShapeDtypeStruct((length, 2 * VAL), BF16),
            jax.ShapeDtypeStruct((8, length), F32),
            jax.ShapeDtypeStruct((length, 128), F32),
        ],
        in_specs=[part(qt), part(q), whole(kt), whole(k), whole(v)],
        out_specs=[
            pl.BlockSpec((BLOCK, 2 * VAL), lambda i: (i, 0)),
            pl.BlockSpec((8, BLOCK), lambda i: (0, i)),
            pl.BlockSpec((BLOCK, 128), lambda i: (i, 0)),
        ],
        compiler_params=pltpu.CompilerParams(vmem_limit_bytes=VMEM_LIMIT),
    )(qt, q, kt, k, v)
    return out, lse, att, q, k, v


def attend_backward_kernel(q_ref, k_ref, v_ref, g_ref, kT_ref, lse_ref, delta_ref, dqT_ref, dk_ref, dv_ref, acc_ref):
    i = pl.program_id(0)
    scale = KEY**-0.5
    s = dot(k_ref[...], q_ref[...], ((1,), (1,))) * scale
    w = jnp.exp(s - lse_ref[0:1, :])
    dp = dot(v_ref[...], g_ref[...], ((1,), (1,)))
    ds = (w * (dp - delta_ref[0:1, :]) * scale).astype(BF16)
    dk_ref[...] = dot(ds, q_ref[...], ((1,), (0,))).astype(BF16)
    dv_ref[...] = dot(w.astype(BF16), g_ref[...], ((1,), (0,))).astype(BF16)
    dq = dot(kT_ref[...], ds, ((1,), (0,)))

    @pl.when(i == 0)
    def _():
        acc_ref[...] = dq

    @pl.when(i > 0)
    def _():
        acc_ref[...] += dq

    @pl.when(i == pl.num_programs(0) - 1)
    def _():
        dqT_ref[...] = acc_ref[...].astype(BF16)


def attend_backward(q, k, v, grad, lse, att):
    length = q.shape[0]
    delta = jnp.sum(grad.astype(F32) * att[:, :VAL], axis=1)
    delta = jnp.broadcast_to(delta[None, :], (8, length))
    kT = k.T
    v = v[:, :VAL]
    whole = lambda a: pl.BlockSpec(a.shape, lambda i: (0, 0))
    part = lambda a: pl.BlockSpec((BLOCK, a.shape[1]), lambda i: (i, 0))
    dqT, dk, dv = pl.pallas_call(
        attend_backward_kernel,
        grid=(length // BLOCK,),
        out_shape=[
            jax.ShapeDtypeStruct((KEY, length), BF16),
            jax.ShapeDtypeStruct((length, KEY), BF16),
            jax.ShapeDtypeStruct((length, VAL), BF16),
        ],
        in_specs=[
            whole(q),
            part(k),
            part(v),
            whole(grad),
            pl.BlockSpec((KEY, BLOCK), lambda i: (0, i)),
            whole(lse),
            whole(delta),
        ],
        out_specs=[
            pl.BlockSpec((KEY, length), lambda i: (0, 0)),
            pl.BlockSpec((BLOCK, KEY), lambda i: (i, 0)),
            pl.BlockSpec((BLOCK, VAL), lambda i: (i, 0)),
        ],
        scratch_shapes=[pltpu.VMEM((KEY, length), F32)],
        compiler_params=pltpu.CompilerParams(vmem_limit_bytes=VMEM_LIMIT),
    )(q, k, v, grad, kT, lse, delta)
    return dqT.T, dk, dv


def gelu_pair(values):
    return jax.jvp(jax.nn.gelu, (values,), (jnp.ones_like(values),))


def neighbours(step):
    pairs = []
    for ctx in range(32):
        for head in range(8):
            j = chunk_of(ctx, head)
            if 0 <= j + step < 8:
                to = member(ctx, head, j + step)
                pairs.append((ctx * 8 + head, to[0] * 8 + to[1]))
    return pairs


def extended(cells):
    up = lax.ppermute(cells[..., -DMAX:, :], ("ctx", "head"), neighbours(1))
    down = lax.ppermute(cells[..., :DMAX, :], ("ctx", "head"), neighbours(-1))
    return jnp.concatenate([up, cells, down], axis=-2)


def per_device(
    window_input,
    norm_gain,
    w_query,
    w_key,
    w_value,
    w_out,
    conv_weight,
    point_weight,
    dilations,
    tangent_query,
    tangent_key,
    curvature,
):
    features = window_input.shape[2]
    ctx, head = me()
    j = chunk_of(ctx, head)
    curves = jnp.pad(curvature[:, None, :], ((0, 0), (0, 7), (0, 64)))
    x_home, c_home = exchange([window_input, curves], [home_stream, home_stream], 0)
    inputs = x_home.reshape(256, features).astype(F32)
    curve = c_home[:, 0, :64].reshape(256, 1)
    spread = jnp.sqrt(jnp.mean(inputs * inputs, axis=-1, keepdims=True) + 1e-06)
    normed = (inputs / spread * norm_gain).astype(BF16)
    normed_all = gather(normed, 1).reshape(2048, features)

    def columns(weight, size):
        return lax.dynamic_slice_in_dim(weight, j * size, size, 1)

    joined = jnp.concatenate(
        [
            columns(w_query, KEY),
            columns(tangent_query, KEY),
            columns(w_key, KEY),
            columns(tangent_key, KEY),
            columns(w_value, VAL),
        ],
        axis=1,
    )
    proj = jnp.dot(normed_all, joined, preferred_element_type=F32).astype(BF16)
    out, lse, att, q, k, v = attend_forward(proj)
    (attended,) = exchange([out.reshape(8, 256, 2 * VAL)], [group_stream], 2)
    out_weight = w_out.reshape((HEADS, VAL, features))
    mixed = inputs + jnp.einsum("hlv,hvc->lc", attended[..., :VAL], out_weight, preferred_element_type=F32)
    tangent_mixed = jnp.einsum("hlv,hvc->lc", attended[..., VAL:], out_weight, preferred_element_type=F32)
    slopes = []
    for layer in range(2):
        dilation = dilations[layer]
        activated, act_slope = gelu_pair(mixed)
        stacked = jnp.stack([activated.astype(BF16), (act_slope * tangent_mixed).astype(BF16)])
        padded = extended(stacked)
        inner = 0.0
        for tap in range(3):
            window = lax.dynamic_slice_in_dim(padded, DMAX + (tap - 1) * dilation, 256, 1)
            inner = inner + jnp.einsum("slc,cf->slf", window, conv_weight[layer, tap], preferred_element_type=F32)
        hidden_value, hidden_slope = gelu_pair(inner[0])
        hidden = jnp.stack([hidden_value.astype(BF16), (hidden_slope * inner[1]).astype(BF16)])
        pointwise = jnp.einsum("slf,fc->slc", hidden, point_weight[layer], preferred_element_type=F32)
        mixed = mixed + pointwise[0]
        tangent_mixed = tangent_mixed + pointwise[1]
        slopes.append((act_slope, hidden_slope, dilation))
    output_tangent = tangent_mixed.astype(BF16)
    gradient = curve * tangent_mixed
    for layer in (1, 0):
        act_slope, hidden_slope, dilation = slopes[layer]
        grad_inner = (
            jnp.einsum("lc,fc->lf", gradient.astype(BF16), point_weight[layer], preferred_element_type=F32)
            * hidden_slope
        ).astype(BF16)
        padded = extended(grad_inner)
        grad_act = 0.0
        for tap in range(3):
            window = lax.dynamic_slice_in_dim(padded, DMAX - (tap - 1) * dilation, 256, 0)
            grad_act = grad_act + jnp.einsum("lf,cf->lc", window, conv_weight[layer, tap], preferred_element_type=F32)
        gradient = gradient + grad_act * act_slope
    grad_attended = jnp.einsum("lc,hvc->hlv", gradient.astype(BF16), out_weight, preferred_element_type=F32).astype(
        BF16
    )
    (grad_item,) = exchange([grad_attended], [group_stream], 3)
    dq, dk, dv = attend_backward(q, k, v, grad_item.reshape(2048, VAL), lse, att)
    pair = jnp.concatenate([dq, dk], axis=1)
    part = lax.dot_general(normed_all, pair, (((0,), (0,)), ((), ())), preferred_element_type=F32)
    grads, parts = exchange(
        [jnp.concatenate([pair, dv], axis=1).reshape(8, 256, 2 * KEY + VAL), part.reshape(32, 24, 2 * KEY)],
        [group_stream, plane_stream],
        4,
    )
    summed = jnp.sum(parts, axis=0) / (32.0 * 2048.0)
    joined_grad = jnp.concatenate(
        [
            w_query.reshape(features, HEADS, KEY),
            w_key.reshape(features, HEADS, KEY),
            w_value.reshape(features, HEADS, VAL),
        ],
        axis=2,
    )
    grad_normed = jnp.einsum("hld,chd->lc", grads, joined_grad, preferred_element_type=F32)
    gained = grad_normed * norm_gain
    input_cotangent = (
        gradient
        + gained / spread
        - inputs * jnp.sum(gained * inputs, axis=-1, keepdims=True) / (features * spread * spread * spread)
    ).astype(BF16)
    out_t, out_c, rows = exchange(
        [
            output_tangent.reshape(4, 64, features),
            input_cotangent.reshape(4, 64, features),
            summed.reshape(8, 3, 2 * KEY),
        ],
        [owner_stream, owner_stream, rows_stream],
        5,
    )
    gv_query = rows[:, :, :KEY].transpose(1, 0, 2).reshape(3, HEADS * KEY)
    gv_key = rows[:, :, KEY:].transpose(1, 0, 2).reshape(3, HEADS * KEY)
    return out_t, out_c, gv_query, gv_key


def solution(mesh):
    in_specs = (P("head", "ctx", None),) + (P(),) * 10 + (P("head", "ctx"),)
    out_specs = (
        P("head", "ctx", None),
        P("head", "ctx", None),
        P(("ctx", "head"), None),
        P(("ctx", "head"), None),
    )
    return jax.shard_map(per_device, mesh=mesh, in_specs=in_specs, out_specs=out_specs, check_vma=False)
```

```python
import functools

import jax
import jax.numpy as jnp
from jax import lax
from jax.experimental import pallas as pl
from jax.experimental.pallas import tpu as pltpu
from jax.sharding import PartitionSpec as P

HEADS = 8
KEY = 64
VAL = 96
DMAX = 16
MESH = pl.DeviceIdType.MESH
VMEM_LIMIT = 56 * 2**20
F32 = jnp.float32
BF16 = jnp.bfloat16
BLOCK = 256


def place(ctx, head):
    return ctx // 8, (ctx // 4) % 2 * 4 + head // 2, ctx % 4, head % 2


def device(y, z, x, core):
    return y * 8 + z // 4 * 4 + x, z % 4 * 2 + core


def chunk_of(ctx, head):
    y, _, x, core = place(ctx, head)
    return (x + 4 - y) % 4 * 2 + core


def member(ctx, head, j):
    y, z, _, _ = place(ctx, head)
    return device(y, z, (j // 2 + y) % 4, j % 2)


def home_of(ctx, head, b):
    y, z, _, core = place(ctx, head)
    return device(b, core * 4 + (z % 4 + 2) % 4, (y + b) % 4, z // 4)


def owner_of(ctx, head, x0):
    y, z, x, core = place(ctx, head)
    return device((x + 4 - y) % 4, core * 4 + (z % 4 + 2) % 4, x0, z // 4)


def me():
    return lax.axis_index("ctx"), lax.axis_index("head")


def signal(barrier, target):
    pl.semaphore_signal(barrier, inc=1, device_id=target, device_id_type=MESH)


def remote(src, dst, send, recv, target):
    return pltpu.make_async_remote_copy(
        src_ref=src, dst_ref=dst, send_sem=send, recv_sem=recv, device_id=target, device_id_type=MESH
    )


class Stream:
    def __init__(self, count, dst, src, slot, own):
        self.count, self.dst, self.src, self.slot, self.own = count, dst, src, slot, own


def home_stream():
    ctx, head = me()
    return Stream(4, lambda i: home_of(ctx, head, i), lambda k: owner_of(ctx, head, k), ctx % 4, None)


def owner_stream():
    ctx, head = me()
    return Stream(4, lambda i: owner_of(ctx, head, i), lambda k: home_of(ctx, head, k), ctx // 8, None)


def group_stream():
    ctx, head = me()
    return Stream(
        8, lambda i: member(ctx, head, i), lambda k: member(ctx, head, k), chunk_of(ctx, head), chunk_of(ctx, head)
    )


def plane_stream():
    ctx, head = me()
    y, z, _, _ = place(ctx, head)
    j = chunk_of(ctx, head)

    def at(r):
        y_at = (r // 8 + 3) % 4
        return device(y_at, r % 8, (j // 2 + y_at) % 4, j % 2)

    rank = (y + 1) % 4 * 8 + z
    return Stream(32, at, at, rank, rank)


def rows_stream():
    ctx, head = me()
    y, z, _, _ = place(ctx, head)
    r = (y + 1) % 4 * 8 + z

    def src(k):
        row = ctx // 8
        y_src = (row + 3) % 4
        return device(y_src, ctx % 8, (k // 2 + y_src) % 4, k % 2)

    return Stream(8, lambda i: (r, i), src, chunk_of(ctx, head), None)


def exchange(arrays, kinds, collective_id):
    count = len(arrays)

    def kernel(*refs):
        xs, outs, sems = refs[:count], refs[count : 2 * count], refs[2 * count :]
        streams = [kind() for kind in kinds]
        barrier = pltpu.get_barrier_semaphore()
        total = 0
        for stream in streams:
            first = 0 if stream.own is None else 1
            base = 0 if stream.own is None else stream.own

            def greet(i, carry, stream=stream, base=base):
                signal(barrier, stream.src((base + i) % stream.count))
                return carry

            lax.fori_loop(first, stream.count, greet, 0)
            total += stream.count - first
        pl.semaphore_wait(barrier, total)
        for n, stream in enumerate(streams):
            x_ref, o_ref, send, recv = xs[n], outs[n], sems[2 * n], sems[2 * n + 1]
            first = 0 if stream.own is None else 1
            base = stream.slot if stream.own is None else stream.own

            def start(i, carry, stream=stream, base=base, x_ref=x_ref, o_ref=o_ref, send=send, recv=recv):
                k = (base + i) % stream.count
                remote(x_ref.at[k], o_ref.at[stream.slot], send.at[k], recv.at[stream.slot], stream.dst(k)).start()
                return carry

            lax.fori_loop(first, stream.count, start, 0)
            if first:
                local = pltpu.make_async_copy(x_ref.at[base], o_ref.at[base], send.at[base])
                local.start()
                local.wait()
        for n, stream in enumerate(streams):
            x_ref, o_ref, send, recv = xs[n], outs[n], sems[2 * n], sems[2 * n + 1]
            first = 0 if stream.own is None else 1
            base = stream.slot if stream.own is None else stream.own

            def finish(i, carry, stream=stream, base=base, x_ref=x_ref, o_ref=o_ref, send=send, recv=recv):
                k = (base + i) % stream.count
                remote(x_ref.at[k], o_ref.at[k], send.at[k], recv.at[k], stream.dst(k)).wait()
                return carry

            lax.fori_loop(first, stream.count, finish, 0)

    scratch = []
    for array in arrays:
        scratch += [pltpu.SemaphoreType.DMA((array.shape[0],))] * 2
    return pl.pallas_call(
        kernel,
        out_shape=[jax.ShapeDtypeStruct(a.shape, a.dtype) for a in arrays],
        in_specs=[pl.BlockSpec(memory_space=pl.ANY)] * count,
        out_specs=[pl.BlockSpec(memory_space=pl.ANY)] * count,
        scratch_shapes=scratch,
        compiler_params=pltpu.CompilerParams(collective_id=collective_id, has_side_effects=True),
    )(*arrays)


def gather(rows, collective_id):
    def kernel(x_ref, o_ref, send, recv, fsend, frecv, local):
        ctx, head = me()
        j = chunk_of(ctx, head)
        core = j % 2
        sibling = member(ctx, head, j - core + 1 - core)
        barrier = pltpu.get_barrier_semaphore()
        signal(barrier, sibling)
        for d in range(1, 4):
            signal(barrier, member(ctx, head, (j + 2 * d) % 8))
        pl.semaphore_wait(barrier, 4)
        for d in range(1, 4):
            remote(x_ref, o_ref.at[j], send.at[d], recv.at[d], member(ctx, head, (j + 2 * d) % 8)).start()
        remote(x_ref, o_ref.at[j], send.at[0], recv.at[0], sibling).start()
        own = pltpu.make_async_copy(x_ref, o_ref.at[j], local)
        own.start()
        for d in (1, 3, 2):
            s = (j + 8 - 2 * d) % 8
            remote(x_ref, o_ref.at[s], send.at[d], recv.at[d], sibling).wait_recv()
            remote(o_ref.at[s], o_ref.at[s], fsend.at[d], frecv.at[d], sibling).start()
        own.wait()
        other = j - core + 1 - core
        remote(x_ref, o_ref.at[other], send.at[0], recv.at[0], sibling).wait()
        for d in (1, 3, 2):
            s = (other + 8 - 2 * d) % 8
            remote(o_ref.at[s], o_ref.at[s], fsend.at[d], frecv.at[d], sibling).wait()
            remote(x_ref, o_ref.at[s], send.at[d], recv.at[d], sibling).wait_send()

    return pl.pallas_call(
        kernel,
        out_shape=jax.ShapeDtypeStruct((8,) + rows.shape, rows.dtype),
        in_specs=[pl.BlockSpec(memory_space=pl.ANY)],
        out_specs=pl.BlockSpec(memory_space=pl.ANY),
        scratch_shapes=[pltpu.SemaphoreType.DMA((4,))] * 4 + [pltpu.SemaphoreType.DMA],
        compiler_params=pltpu.CompilerParams(collective_id=collective_id, has_side_effects=True),
    )(rows)


def dot(a, b, contract):
    return lax.dot_general(a, b, ((contract[0], contract[1]), ((), ())), preferred_element_type=F32)


def attend_forward_kernel(qt_ref, q_ref, kt_ref, k_ref, v_ref, o_ref, lse_ref, att_ref):
    scale = KEY**-0.5
    s = dot(q_ref[...], k_ref[...], ((1,), (1,))) * scale
    top = jnp.max(s, axis=1, keepdims=True)
    p = jnp.exp(s - top)
    ext = dot(p.astype(BF16), v_ref[...], ((1,), (0,)))
    total = ext[:, VAL : VAL + 1]
    inv = 1.0 / total
    ts = dot(qt_ref[...], kt_ref[...], ((1,), (1,))) * scale
    mean = jnp.sum(p * ts, axis=1, keepdims=True) / jnp.sum(p, axis=1, keepdims=True)
    tw = p * (ts - mean)
    tan = dot(tw.astype(BF16), v_ref[...], ((1,), (0,))) * inv
    att = ext * inv
    o_ref[0] = att[:, :VAL].astype(BF16)
    o_ref[1] = tan[:, :VAL].astype(BF16)
    att_ref[...] = att
    lse = jnp.broadcast_to(top + jnp.log(total), (BLOCK, 128))
    lse_ref[...] = lse.T[:8]


def attend_forward(proj):
    length = proj.shape[0]
    q, tq = proj[:, :KEY], proj[:, KEY : 2 * KEY]
    k, tk = proj[:, 2 * KEY : 3 * KEY], proj[:, 3 * KEY : 4 * KEY]
    qt = jnp.concatenate([tq, q], axis=1)
    kt = jnp.concatenate([k, tk], axis=1)
    v = jnp.concatenate([proj[:, 4 * KEY :], jnp.ones((length, 128 - VAL), BF16)], axis=1)
    whole = lambda a: pl.BlockSpec(a.shape, lambda i: (0, 0))
    part = lambda a: pl.BlockSpec((BLOCK, a.shape[1]), lambda i: (i, 0))
    out, lse, att = pl.pallas_call(
        attend_forward_kernel,
        grid=(length // BLOCK,),
        out_shape=[
            jax.ShapeDtypeStruct((2, length, VAL), BF16),
            jax.ShapeDtypeStruct((8, length), F32),
            jax.ShapeDtypeStruct((length, 128), F32),
        ],
        in_specs=[part(qt), part(q), whole(kt), whole(k), whole(v)],
        out_specs=[
            pl.BlockSpec((2, BLOCK, VAL), lambda i: (0, i, 0)),
            pl.BlockSpec((8, BLOCK), lambda i: (0, i)),
            pl.BlockSpec((BLOCK, 128), lambda i: (i, 0)),
        ],
        compiler_params=pltpu.CompilerParams(vmem_limit_bytes=VMEM_LIMIT),
    )(qt, q, kt, k, v)
    return out, lse, att, q, k, v


def attend_backward_kernel(q_ref, k_ref, v_ref, g_ref, kT_ref, lse_ref, delta_ref, dqT_ref, dk_ref, dv_ref, acc_ref):
    i = pl.program_id(0)
    scale = KEY**-0.5
    s = dot(k_ref[...], q_ref[...], ((1,), (1,))) * scale
    w = jnp.exp(s - lse_ref[0:1, :])
    dp = dot(v_ref[...], g_ref[...], ((1,), (1,)))
    ds = (w * (dp - delta_ref[0:1, :]) * scale).astype(BF16)
    dk_ref[...] = dot(ds, q_ref[...], ((1,), (0,))).astype(BF16)
    dv_ref[...] = dot(w.astype(BF16), g_ref[...], ((1,), (0,))).astype(BF16)
    dq = dot(kT_ref[...], ds, ((1,), (0,)))

    @pl.when(i == 0)
    def _():
        acc_ref[...] = dq

    @pl.when(i > 0)
    def _():
        acc_ref[...] += dq

    @pl.when(i == pl.num_programs(0) - 1)
    def _():
        dqT_ref[...] = acc_ref[...].astype(BF16)


def attend_backward(q, k, v, grad, lse, att):
    length = q.shape[0]
    delta = jnp.sum(grad.astype(F32) * att[:, :VAL], axis=1)
    delta = jnp.broadcast_to(delta[None, :], (8, length))
    kT = k.T
    v = v[:, :VAL]
    whole = lambda a: pl.BlockSpec(a.shape, lambda i: (0, 0))
    part = lambda a: pl.BlockSpec((BLOCK, a.shape[1]), lambda i: (i, 0))
    dqT, dk, dv = pl.pallas_call(
        attend_backward_kernel,
        grid=(length // BLOCK,),
        out_shape=[
            jax.ShapeDtypeStruct((KEY, length), BF16),
            jax.ShapeDtypeStruct((length, KEY), BF16),
            jax.ShapeDtypeStruct((length, VAL), BF16),
        ],
        in_specs=[
            whole(q),
            part(k),
            part(v),
            whole(grad),
            pl.BlockSpec((KEY, BLOCK), lambda i: (0, i)),
            whole(lse),
            whole(delta),
        ],
        out_specs=[
            pl.BlockSpec((KEY, length), lambda i: (0, 0)),
            pl.BlockSpec((BLOCK, KEY), lambda i: (i, 0)),
            pl.BlockSpec((BLOCK, VAL), lambda i: (i, 0)),
        ],
        scratch_shapes=[pltpu.VMEM((KEY, length), F32)],
        compiler_params=pltpu.CompilerParams(vmem_limit_bytes=VMEM_LIMIT),
    )(q, k, v, grad, kT, lse, delta)
    return dqT.T, dk, dv


def gelu_pair(v):
    root = 0.7978845608028654
    square = v * v
    t = jnp.tanh(root * (v + 0.044715 * v * square))
    half = 0.5 * (1.0 + t)
    return v * half, half + 0.5 * v * (1.0 - t * t) * (root + (3.0 * 0.044715 * root) * square)


def picker(dilation, rows):
    shape = (2 * rows, rows + 2 * DMAX)
    row = lax.broadcasted_iota(jnp.int32, shape, 0)
    column = lax.broadcasted_iota(jnp.int32, shape, 1)
    wanted = jnp.where(row < rows, row + DMAX - dilation, row - rows + DMAX + dilation)
    return jnp.where(column == wanted, 1.0, 0.0).astype(BF16)


def conv_kernel(
    dil_ref,
    att_ref,
    x_ref,
    curve_ref,
    w_out_ref,
    conv_ref,
    point_ref,
    tan_out_ref,
    grad_out_ref,
    item_ref,
    mixed_ref,
    tan_ref,
    slope_ref,
    hslope_ref,
    pad_ref,
    gpad_ref,
    edge_ref,
    halo_ref,
    gedge_ref,
    ghalo_ref,
    out_ref,
    ga_ref,
    h_send,
    h_recv,
    o_send,
    o_recv,
    g_send,
    g_recv,
):
    ctx, head = me()
    j = chunk_of(ctx, head)
    rows = x_ref.shape[0]
    barrier = pltpu.get_barrier_semaphore()

    def beside(step):
        return member(ctx, head, (j + step + 8) % 8)

    @pl.when(j > 0)
    def _():
        signal(barrier, beside(-1))

    @pl.when(j < 7)
    def _():
        signal(barrier, beside(1))

    owners = owner_stream()
    group = group_stream()
    for k in range(4):
        signal(barrier, owners.src(k))
    for k in range(1, 8):
        signal(barrier, group.src((j + k) % 8))

    def swap(n, edge, halo, pad, width):
        lead = pad.shape[:-2]
        edge[0] = pad[..., DMAX : 2 * DMAX, :]
        edge[1] = pad[..., rows : rows + DMAX, :]
        down = remote(edge.at[0], halo.at[1], h_send.at[2 * n], h_recv.at[2 * n], beside(-1))
        up = remote(edge.at[1], halo.at[0], h_send.at[2 * n + 1], h_recv.at[2 * n + 1], beside(1))

        @pl.when(j > 0)
        def _():
            down.start()

        @pl.when(j < 7)
        def _():
            up.start()

        def finish():
            @pl.when(j > 0)
            def _():
                up.wait_recv()
                pad[..., 0:DMAX, :] = halo[0]
                down.wait_send()

            @pl.when(j == 0)
            def _():
                pad[..., 0:DMAX, :] = jnp.zeros(lead + (DMAX, width), BF16)

            @pl.when(j < 7)
            def _():
                down.wait_recv()
                pad[..., rows + DMAX : rows + 2 * DMAX, :] = halo[1]
                up.wait_send()

            @pl.when(j == 7)
            def _():
                pad[..., rows + DMAX : rows + 2 * DMAX, :] = jnp.zeros(lead + (DMAX, width), BF16)

        return finish

    both = jnp.zeros((2 * rows, x_ref.shape[1]), F32)
    for h in range(HEADS):
        both = both + dot(
            att_ref[h].reshape(2 * rows, VAL), w_out_ref[h * VAL : (h + 1) * VAL, :], ((1,), (0,))
        )
    mixed_ref[...] = x_ref[...].astype(F32) + both[:rows]
    tan_ref[...] = both[rows:]
    ends = jnp.where((j == 0) | (j == 7), 1, 2)
    pl.semaphore_wait(barrier, 11 + ends)
    features = x_ref.shape[1]
    width = conv_ref.shape[3]
    for layer in range(2):
        dilation = dil_ref[layer]
        act, slope = gelu_pair(mixed_ref[...])
        slope_ref[layer] = slope
        pad_ref[0, DMAX : DMAX + rows, :] = act.astype(BF16)
        pad_ref[1, DMAX : DMAX + rows, :] = (slope * tan_ref[...]).astype(BF16)
        finish = swap(layer, edge_ref.at[layer], halo_ref.at[layer], pad_ref, features)

        inner = dot(
            pad_ref[:, DMAX : DMAX + rows, :].reshape(2 * rows, features), conv_ref[layer, 1], ((1,), (0,))
        )
        finish()
        pick = picker(dilation, rows)
        value = dot(pick, pad_ref[0], ((1,), (0,))).astype(BF16)
        tangent = dot(pick, pad_ref[1], ((1,), (0,))).astype(BF16)
        for n, tap in ((0, 0), (1, 2)):
            window = jnp.concatenate([value[n * rows : (n + 1) * rows], tangent[n * rows : (n + 1) * rows]], axis=0)
            inner = inner + dot(window, conv_ref[layer, tap], ((1,), (0,)))
        hidden, hslope = gelu_pair(inner[:rows])
        hslope_ref[layer] = hslope
        hidden = jnp.concatenate([hidden, hslope * inner[rows:]], axis=0).astype(BF16)
        point = dot(hidden, point_ref[layer], ((1,), (0,)))
        if layer == 0:
            mixed_ref[...] += point[:rows]
        tan_ref[...] += point[rows:]
    out_ref[...] = tan_ref[...].astype(BF16)
    sends = []
    for k in range(4):
        sends.append(
            remote(
                out_ref.at[pl.ds(64 * k, 64)], tan_out_ref.at[owners.slot], o_send.at[k], o_recv.at[owners.slot], owners.dst(k)
            )
        )
        sends[-1].start()
    grad_out_ref[...] = curve_ref[...] * tan_ref[...]
    for layer in (1, 0):
        dilation = dil_ref[layer]
        back = dot(grad_out_ref[...].astype(BF16), point_ref[layer], ((1,), (1,)))
        gpad_ref[DMAX : DMAX + rows, :] = (back * hslope_ref[layer]).astype(BF16)
        finish = swap(2 + layer, gedge_ref.at[layer], ghalo_ref.at[layer], gpad_ref, width)

        act = dot(gpad_ref[DMAX : DMAX + rows, :], conv_ref[layer, 1], ((1,), (1,)))
        finish()
        windows = dot(picker(dilation, rows), gpad_ref[...], ((1,), (0,))).astype(BF16)
        act = act + dot(windows[:rows], conv_ref[layer, 2], ((1,), (1,)))
        act = act + dot(windows[rows:], conv_ref[layer, 0], ((1,), (1,)))
        grad_out_ref[...] += slope_ref[layer] * act
    final = grad_out_ref[...].astype(BF16)
    for h in range(HEADS):
        ga_ref[h] = dot(final, w_out_ref[h * VAL : (h + 1) * VAL, :], ((1,), (1,))).astype(BF16)

    def start(k, carry):
        i = (j + k) % 8
        remote(ga_ref.at[i], item_ref.at[j], g_send.at[i], g_recv.at[j], group.dst(i)).start()
        return carry

    lax.fori_loop(1, 8, start, 0)
    own = pltpu.make_async_copy(ga_ref.at[j], item_ref.at[j], g_send.at[j])
    own.start()
    own.wait()

    def end(k, carry):
        i = (j + k) % 8
        remote(ga_ref.at[i], item_ref.at[i], g_send.at[i], g_recv.at[i], group.dst(i)).wait()
        return carry

    lax.fori_loop(1, 8, end, 0)
    for k in range(4):
        sends[k].wait_send()
        remote(out_ref.at[pl.ds(64 * k, 64)], tan_out_ref.at[k], o_send.at[k], o_recv.at[k], owners.dst(k)).wait_recv()


def conv_chain(dilations, attended, x_home, curve, w_out, conv_weight, point_weight, collective_id):
    rows, features = x_home.shape
    width = conv_weight.shape[3]
    vmem = pl.BlockSpec(memory_space=pltpu.VMEM)
    anywhere = pl.BlockSpec(memory_space=pl.ANY)
    return pl.pallas_call(
        conv_kernel,
        out_shape=[
            jax.ShapeDtypeStruct((4, 64, features), BF16),
            jax.ShapeDtypeStruct((rows, features), F32),
            jax.ShapeDtypeStruct((8, rows, VAL), BF16),
        ],
        in_specs=[pl.BlockSpec(memory_space=pltpu.SMEM)] + [vmem] * 6,
        out_specs=[anywhere, vmem, anywhere],
        scratch_shapes=[
            pltpu.VMEM((rows, features), F32),
            pltpu.VMEM((rows, features), F32),
            pltpu.VMEM((2, rows, features), F32),
            pltpu.VMEM((2, rows, width), F32),
            pltpu.VMEM((2, rows + 2 * DMAX, features), BF16),
            pltpu.VMEM((rows + 2 * DMAX, width), BF16),
            pltpu.VMEM((2, 2, 2, DMAX, features), BF16),
            pltpu.VMEM((2, 2, 2, DMAX, features), BF16),
            pltpu.VMEM((2, 2, DMAX, width), BF16),
            pltpu.VMEM((2, 2, DMAX, width), BF16),
            pltpu.VMEM((rows, features), BF16),
            pltpu.VMEM((8, rows, VAL), BF16),
            pltpu.SemaphoreType.DMA((8,)),
            pltpu.SemaphoreType.DMA((8,)),
            pltpu.SemaphoreType.DMA((4,)),
            pltpu.SemaphoreType.DMA((4,)),
            pltpu.SemaphoreType.DMA((8,)),
            pltpu.SemaphoreType.DMA((8,)),
        ],
        compiler_params=pltpu.CompilerParams(
            collective_id=collective_id, has_side_effects=True, vmem_limit_bytes=VMEM_LIMIT
        ),
    )(dilations, attended, x_home, curve, w_out, conv_weight, point_weight)


def final_kernel(
    x_ref, grad_ref, gain_ref, pair_ref, dv_ref, wq_ref, wk_ref, wv_ref, parts_ref,
    out_c_ref, gvq_ref, gvk_ref,
    buf_ref, rows_ref, got_ref, o_send, o_recv, r_send, r_recv,
):
    ctx, head = me()
    owners = owner_stream()
    rows = rows_stream()
    barrier = pltpu.get_barrier_semaphore()
    for k in range(4):
        signal(barrier, owners.src(k))
    for k in range(8):
        signal(barrier, rows.src(k))
    summed = jnp.sum(parts_ref[...], axis=0) * (1.0 / (32.0 * 2048.0))
    for k in range(8):
        rows_ref[k, 0:3, :] = summed[3 * k : 3 * k + 3, :]
        rows_ref[k, 3:8, :] = jnp.zeros((5, 2 * KEY), F32)
    pl.semaphore_wait(barrier, 12)
    for k in range(8):
        remote(rows_ref.at[k], got_ref.at[rows.slot], r_send.at[k], r_recv.at[rows.slot], rows.dst(k)).start()
    inputs = x_ref[...].astype(F32)
    count, features = inputs.shape
    acc = jnp.zeros((count, features), F32)
    for h in range(HEADS):
        w = jnp.concatenate([wq_ref[:, h * KEY : (h + 1) * KEY], wk_ref[:, h * KEY : (h + 1) * KEY]], axis=1)
        acc = acc + dot(pair_ref[h], w, ((1,), (1,)))
        acc = acc + dot(dv_ref[h], wv_ref[:, h * VAL : (h + 1) * VAL], ((1,), (1,)))
    gained = acc * gain_ref[...]
    spread = jnp.sqrt(jnp.mean(inputs * inputs, axis=-1, keepdims=True) + 1e-06)
    along = jnp.sum(gained * inputs, axis=-1, keepdims=True)
    inv = 1.0 / spread
    buf_ref[...] = (
        grad_ref[...] + gained * inv - inputs * (along / (features * spread * spread * spread))
    ).astype(BF16)
    for k in range(4):
        remote(
            buf_ref.at[pl.ds(64 * k, 64)], out_c_ref.at[owners.slot], o_send.at[k], o_recv.at[owners.slot], owners.dst(k)
        ).start()
    for k in range(8):
        remote(rows_ref.at[k], got_ref.at[k], r_send.at[k], r_recv.at[k], rows.dst(k)).wait()
    for k in range(8):
        gvq_ref[:, k * KEY : (k + 1) * KEY] = got_ref[k, 0:3, :KEY]
        gvk_ref[:, k * KEY : (k + 1) * KEY] = got_ref[k, 0:3, KEY:]
    for k in range(4):
        remote(
            buf_ref.at[pl.ds(64 * k, 64)], out_c_ref.at[k], o_send.at[k], o_recv.at[k], owners.dst(k)
        ).wait()


def finish_rows(x_home, gradient, norm_gain, pair, dv, wq, wk, wv, parts, collective_id):
    rows, features = x_home.shape
    vmem = pl.BlockSpec(memory_space=pltpu.VMEM)
    return pl.pallas_call(
        final_kernel,
        out_shape=[
            jax.ShapeDtypeStruct((4, 64, features), BF16),
            jax.ShapeDtypeStruct((3, HEADS * KEY), F32),
            jax.ShapeDtypeStruct((3, HEADS * KEY), F32),
        ],
        in_specs=[vmem] * 9,
        out_specs=[pl.BlockSpec(memory_space=pl.ANY), vmem, vmem],
        scratch_shapes=[
            pltpu.VMEM((rows, features), BF16),
            pltpu.VMEM((8, 8, 2 * KEY), F32),
            pltpu.VMEM((8, 8, 2 * KEY), F32),
            pltpu.SemaphoreType.DMA((4,)),
            pltpu.SemaphoreType.DMA((4,)),
            pltpu.SemaphoreType.DMA((8,)),
            pltpu.SemaphoreType.DMA((8,)),
        ],
        compiler_params=pltpu.CompilerParams(
            collective_id=collective_id, has_side_effects=True, vmem_limit_bytes=VMEM_LIMIT
        ),
    )(x_home, gradient, norm_gain, pair, dv, wq, wk, wv, parts)


def per_device(
    window_input,
    norm_gain,
    w_query,
    w_key,
    w_value,
    w_out,
    conv_weight,
    point_weight,
    dilations,
    tangent_query,
    tangent_key,
    curvature,
):
    features = window_input.shape[2]
    ctx, head = me()
    j = chunk_of(ctx, head)
    curves = jnp.pad(curvature[:, None, :], ((0, 0), (0, 7), (0, 64)))
    x_home, c_home = exchange([window_input, curves], [home_stream, home_stream], 0)
    inputs = x_home.reshape(256, features).astype(F32)
    curve = c_home[:, 0, :64].reshape(256, 1)
    spread = jnp.sqrt(jnp.mean(inputs * inputs, axis=-1, keepdims=True) + 1e-06)
    normed = (inputs / spread * norm_gain).astype(BF16)
    normed_all = gather(normed, 1).reshape(2048, features)

    def columns(weight, size):
        return lax.dynamic_slice_in_dim(weight, j * size, size, 1)

    joined = jnp.concatenate(
        [
            columns(w_query, KEY),
            columns(tangent_query, KEY),
            columns(w_key, KEY),
            columns(tangent_key, KEY),
            columns(w_value, VAL),
        ],
        axis=1,
    )
    proj = jnp.dot(normed_all, joined, preferred_element_type=F32).astype(BF16)
    out, lse, att, q, k, v = attend_forward(proj)
    (attended,) = exchange([out.reshape(2, 8, 256, VAL).transpose(1, 0, 2, 3)], [group_stream], 2)
    out_t, gradient, grad_item = conv_chain(
        dilations, attended, x_home.reshape(256, features), curve, w_out, conv_weight, point_weight, 3
    )
    dq, dk, dv = attend_backward(q, k, v, grad_item.reshape(2048, VAL), lse, att)
    pair = jnp.concatenate([dq, dk], axis=1)
    part = lax.dot_general(normed_all, pair, (((0,), (0,)), ((), ())), preferred_element_type=F32)
    pairs, dvs, parts = exchange(
        [pair.reshape(8, 256, 2 * KEY), dv.reshape(8, 256, VAL), part.reshape(32, 24, 2 * KEY)],
        [group_stream, group_stream, plane_stream],
        4,
    )
    out_c, gv_query, gv_key = finish_rows(
        x_home.reshape(256, features), gradient, norm_gain[None, :], pairs, dvs, w_query, w_key, w_value, parts, 5
    )
    return out_t, out_c, gv_query, gv_key


def solution(mesh):
    in_specs = (P("head", "ctx", None),) + (P(),) * 10 + (P("head", "ctx"),)
    out_specs = (
        P("head", "ctx", None),
        P("head", "ctx", None),
        P(("ctx", "head"), None),
        P(("ctx", "head"), None),
    )
    return jax.shard_map(per_device, mesh=mesh, in_specs=in_specs, out_specs=out_specs, check_vma=False)
```

```python
import jax
import jax.numpy as jnp
from jax import lax
from jax.experimental import pallas as pl
from jax.experimental.pallas import tpu as pltpu
from jax.sharding import PartitionSpec as P

HEADS = 8
KEY = 64
VAL = 96
DMAX = 16
MESH = pl.DeviceIdType.MESH
VMEM_LIMIT = 56 * 2**20
F32 = jnp.float32
BF16 = jnp.bfloat16
BLOCK = 256


def place(ctx, head):
    return ctx // 8, (ctx // 4) % 2 * 4 + head // 2, ctx % 4, head % 2


def device(y, z, x, core):
    return y * 8 + z // 4 * 4 + x, z % 4 * 2 + core


def chunk_of(ctx, head):
    y, _, x, core = place(ctx, head)
    return (x + 4 - y) % 4 * 2 + core


def member(ctx, head, j):
    y, z, _, _ = place(ctx, head)
    return device(y, z, (j // 2 + y) % 4, j % 2)


def home_of(ctx, head, b):
    y, z, _, core = place(ctx, head)
    return device(b, core * 4 + (z % 4 + 2) % 4, (y + b) % 4, z // 4)


def owner_of(ctx, head, x0):
    y, z, x, core = place(ctx, head)
    return device((x + 4 - y) % 4, core * 4 + (z % 4 + 2) % 4, x0, z // 4)


def me():
    return lax.axis_index("ctx"), lax.axis_index("head")


def signal(barrier, target):
    pl.semaphore_signal(barrier, inc=1, device_id=target, device_id_type=MESH)


def remote(src, dst, send, recv, target):
    return pltpu.make_async_remote_copy(
        src_ref=src, dst_ref=dst, send_sem=send, recv_sem=recv, device_id=target, device_id_type=MESH
    )


class Stream:
    def __init__(self, count, dst, src, slot, own):
        self.count, self.dst, self.src, self.slot, self.own = count, dst, src, slot, own


def home_stream():
    ctx, head = me()
    return Stream(4, lambda i: home_of(ctx, head, i), lambda k: owner_of(ctx, head, k), ctx % 4, None)


def owner_stream():
    ctx, head = me()
    return Stream(4, lambda i: owner_of(ctx, head, i), lambda k: home_of(ctx, head, k), ctx // 8, None)


def group_stream():
    ctx, head = me()
    return Stream(
        8, lambda i: member(ctx, head, i), lambda k: member(ctx, head, k), chunk_of(ctx, head), chunk_of(ctx, head)
    )


def plane_stream():
    ctx, head = me()
    y, z, _, _ = place(ctx, head)
    j = chunk_of(ctx, head)

    def at(r):
        y_at = (r // 8 + 3) % 4
        return device(y_at, r % 8, (j // 2 + y_at) % 4, j % 2)

    rank = (y + 1) % 4 * 8 + z
    return Stream(32, at, at, rank, rank)


def rows_stream():
    ctx, head = me()
    y, z, _, _ = place(ctx, head)
    r = (y + 1) % 4 * 8 + z

    def src(k):
        row = ctx // 8
        y_src = (row + 3) % 4
        return device(y_src, ctx % 8, (k // 2 + y_src) % 4, k % 2)

    return Stream(8, lambda i: (r, i), src, chunk_of(ctx, head), None)


def dot(a, b, contract):
    return lax.dot_general(a, b, ((contract[0], contract[1]), ((), ())), preferred_element_type=F32)


def front_kernel(
    x_ref, c_ref, gain_ref, wq_ref, tq_ref, wk_ref, tk_ref, wv_ref,
    home_ref, curve_ref, all_ref, qt_ref, kt_ref, v_ref,
    join_ref, x_send, x_recv, c_send, c_recv, send, recv,
):
    ctx, head = me()
    j = chunk_of(ctx, head)
    core = j % 2
    homes = home_stream()
    barrier = pltpu.get_barrier_semaphore()
    sibling = j + 1 - 2 * core
    up, down = (j + 2) % 8, (j + 6) % 8
    for k in range(4):
        signal(barrier, homes.src(k))
    for i in (sibling, up, down):
        signal(barrier, member(ctx, head, i))
    pl.semaphore_wait(barrier, 7)
    for k in range(4):
        remote(x_ref.at[k], home_ref.at[homes.slot], x_send.at[k], x_recv.at[homes.slot], homes.dst(k)).start()
        remote(c_ref.at[k], curve_ref.at[homes.slot], c_send.at[k], c_recv.at[homes.slot], homes.dst(k)).start()

    def columns(weight, size, at):
        shape = (weight.shape[1], 384)
        row = lax.broadcasted_iota(jnp.int32, shape, 0)
        column = lax.broadcasted_iota(jnp.int32, shape, 1)
        hit = (row - j * size == column - at) & (column >= at) & (column < at + size)
        return dot(weight[...], jnp.where(hit, 1.0, 0.0).astype(BF16), ((1,), (0,)))

    joined = columns(tq_ref, KEY, 0) + columns(wq_ref, KEY, KEY)
    joined = joined + columns(wk_ref, KEY, 2 * KEY) + columns(tk_ref, KEY, 3 * KEY)
    joined = joined + columns(wv_ref, VAL, 4 * KEY)
    join_ref[...] = joined.astype(BF16)

    def piece(i, p):
        return all_ref.at[i, pl.ds(64 * p, 64)]

    def push(i, p, way, to):
        remote(piece(i, p), piece(i, p), send.at[i, p, way], recv.at[i, p], member(ctx, head, to)).start()

    def arrived(i, p):
        remote(piece(i, p), piece(i, p), send.at[i, p, 0], recv.at[i, p], member(ctx, head, sibling)).wait_recv()

    def sent(i, p, way, to):
        remote(piece(i, p), piece(i, p), send.at[i, p, way], recv.at[i, p], member(ctx, head, to)).wait_send()

    for p in range(4):
        remote(x_ref.at[p], home_ref.at[p], x_send.at[p], x_recv.at[p], homes.dst(p)).wait_recv()
        inputs = home_ref[p].astype(F32)
        spread = jnp.sqrt(jnp.mean(inputs * inputs, axis=-1, keepdims=True) + 1e-06)
        all_ref[j, 64 * p : 64 * p + 64, :] = (inputs / spread * gain_ref[...]).astype(BF16)
        push(j, p, 1, up)
        push(j, p, 2, down)
        push(j, p, 0, sibling)

    def project(i):
        rows = pl.ds(pl.multiple_of(i * 256, 256), 256)
        proj = dot(all_ref[i], join_ref[...], ((1,), (0,))).astype(BF16)
        qt_ref[rows, :] = proj[:, :128]
        kt_ref[rows, :] = proj[:, 128:256]
        lane = lax.broadcasted_iota(jnp.int32, (256, 128), 1)
        v_ref[rows, :] = jnp.where(lane < VAL, proj[:, 256:].astype(F32), 1.0).astype(BF16)

    for p in range(4):
        arrived(down, p)
        if p < 2:
            push(down, p, 1, up)
        push(down, p, 0, sibling)
        arrived(up, p)
        if p >= 2:
            push(up, p, 2, down)
        push(up, p, 0, sibling)
    project(j)
    project(down)
    project(up)
    far = (j + 4) % 8
    for p in (0, 2, 1, 3):
        arrived(far, p)
        push(far, p, 0, sibling)
    project(far)
    for d in (0, 2, 6, 4):
        i = (sibling + d) % 8
        for p in range(4):
            arrived(i, p)
        project(i)
    for k in range(4):
        remote(x_ref.at[k], home_ref.at[k], x_send.at[k], x_recv.at[k], homes.dst(k)).wait_send()
        remote(c_ref.at[k], curve_ref.at[k], c_send.at[k], c_recv.at[k], homes.dst(k)).wait()
    for p in range(4):
        sent(j, p, 1, up)
        sent(j, p, 2, down)
        for i in (j, up, down, far):
            sent(i, p, 0, sibling)
        if p < 2:
            sent(down, p, 1, up)
        else:
            sent(up, p, 2, down)


def front(window_input, curves, gain, wq, tq, wk, tk, wv, collective_id):
    features = window_input.shape[2]
    vmem = pl.BlockSpec(memory_space=pltpu.VMEM)
    length = 2048
    return pl.pallas_call(
        front_kernel,
        out_shape=[
            jax.ShapeDtypeStruct((4, 64, features), BF16),
            jax.ShapeDtypeStruct(curves.shape, F32),
            jax.ShapeDtypeStruct((8, 256, features), BF16),
            jax.ShapeDtypeStruct((length, 128), BF16),
            jax.ShapeDtypeStruct((length, 128), BF16),
            jax.ShapeDtypeStruct((length, 128), BF16),
        ],
        in_specs=[vmem] * 8,
        out_specs=[vmem] * 6,
        scratch_shapes=[
            pltpu.VMEM((features, 384), BF16),
            pltpu.SemaphoreType.DMA((4,)),
            pltpu.SemaphoreType.DMA((4,)),
            pltpu.SemaphoreType.DMA((4,)),
            pltpu.SemaphoreType.DMA((4,)),
            pltpu.SemaphoreType.DMA((8, 4, 3)),
            pltpu.SemaphoreType.DMA((8, 4)),
        ],
        compiler_params=pltpu.CompilerParams(
            collective_id=collective_id, has_side_effects=True, vmem_limit_bytes=VMEM_LIMIT
        ),
    )(window_input, curves, gain, wq, tq, wk, tk, wv)


def forward_kernel(qt_ref, kt_ref, v_ref, out_ref, lse_ref, att_ref, buf_ref, send, recv):
    ctx, head = me()
    j = chunk_of(ctx, head)
    scale = KEY**-0.5
    barrier = pltpu.get_barrier_semaphore()
    for d in range(1, 8):
        signal(barrier, member(ctx, head, (j + d) % 8))
    pl.semaphore_wait(barrier, 7)

    def block(t, carry):
        i = (j + 1 + t) % 8
        rows = pl.ds(pl.multiple_of(i * BLOCK, BLOCK), BLOCK)
        qt = qt_ref[rows, :]
        s = dot(qt[:, KEY:], kt_ref[:, :KEY], ((1,), (1,))) * scale
        top = jnp.max(s, axis=1, keepdims=True)
        p = jnp.exp(s - top)
        ext = dot(p.astype(BF16), v_ref[...], ((1,), (0,)))
        total = ext[:, VAL : VAL + 1]
        inv = 1.0 / total
        ts = dot(qt, kt_ref[...], ((1,), (1,))) * scale
        mean = jnp.sum(p * ts, axis=1, keepdims=True) / jnp.sum(p, axis=1, keepdims=True)
        tw = p * (ts - mean)
        tan = dot(tw.astype(BF16), v_ref[...], ((1,), (0,))) * inv
        att = ext * inv
        buf_ref[i, 0] = att[:, :VAL].astype(BF16)
        buf_ref[i, 1] = tan[:, :VAL].astype(BF16)

        @pl.when(t < 7)
        def _():
            remote(buf_ref.at[i], out_ref.at[j], send.at[i], recv.at[j], member(ctx, head, i)).start()

        att_ref[rows, :] = att
        lse_ref[:, rows] = jnp.broadcast_to(top + jnp.log(total), (BLOCK, 128)).T[:8]
        return carry

    lax.fori_loop(0, 8, block, 0)
    own = pltpu.make_async_copy(buf_ref.at[j], out_ref.at[j], send.at[j])
    own.start()
    own.wait()

    def end(t, carry):
        i = (j + 1 + t) % 8
        remote(buf_ref.at[i], out_ref.at[i], send.at[i], recv.at[i], member(ctx, head, i)).wait()
        return carry

    lax.fori_loop(0, 7, end, 0)


def attend_forward(qt, kt, v, collective_id):
    length = qt.shape[0]
    vmem = pl.BlockSpec(memory_space=pltpu.VMEM)
    return pl.pallas_call(
        forward_kernel,
        out_shape=[
            jax.ShapeDtypeStruct((8, 2, BLOCK, VAL), BF16),
            jax.ShapeDtypeStruct((8, length), F32),
            jax.ShapeDtypeStruct((length, 128), F32),
        ],
        in_specs=[vmem] * 3,
        out_specs=[vmem] * 3,
        scratch_shapes=[
            pltpu.VMEM((8, 2, BLOCK, VAL), BF16),
            pltpu.SemaphoreType.DMA((8,)),
            pltpu.SemaphoreType.DMA((8,)),
        ],
        compiler_params=pltpu.CompilerParams(
            collective_id=collective_id, has_side_effects=True, vmem_limit_bytes=VMEM_LIMIT
        ),
    )(qt, kt, v)


def gelu_pair(v):
    root = 0.7978845608028654
    square = v * v
    t = jnp.tanh(root * (v + 0.044715 * v * square))
    half = 0.5 * (1.0 + t)
    return v * half, half + 0.5 * v * (1.0 - t * t) * (root + (3.0 * 0.044715 * root) * square)


def picker(dilation, rows):
    shape = (2 * rows, rows + 2 * DMAX)
    row = lax.broadcasted_iota(jnp.int32, shape, 0)
    column = lax.broadcasted_iota(jnp.int32, shape, 1)
    wanted = jnp.where(row < rows, row + DMAX - dilation, row - rows + DMAX + dilation)
    return jnp.where(column == wanted, 1.0, 0.0).astype(BF16)


def conv_kernel(
    dil_ref,
    att_ref,
    x_ref,
    curve_ref,
    w_out_ref,
    conv_ref,
    point_ref,
    tan_out_ref,
    grad_out_ref,
    item_ref,
    mixed_ref,
    tan_ref,
    slope_ref,
    hslope_ref,
    pad_ref,
    gpad_ref,
    edge_ref,
    halo_ref,
    gedge_ref,
    ghalo_ref,
    out_ref,
    ga_ref,
    h_send,
    h_recv,
    o_send,
    o_recv,
    g_send,
    g_recv,
):
    ctx, head = me()
    j = chunk_of(ctx, head)
    rows = x_ref.shape[0]
    barrier = pltpu.get_barrier_semaphore()

    def beside(step):
        return member(ctx, head, (j + step + 8) % 8)

    @pl.when(j > 0)
    def _():
        signal(barrier, beside(-1))

    @pl.when(j < 7)
    def _():
        signal(barrier, beside(1))

    owners = owner_stream()
    group = group_stream()
    for k in range(4):
        signal(barrier, owners.src(k))
    for k in range(1, 8):
        signal(barrier, group.src((j + k) % 8))

    def swap(n, edge, halo, pad, width):
        lead = pad.shape[:-2]
        edge[0] = pad[..., DMAX : 2 * DMAX, :]
        edge[1] = pad[..., rows : rows + DMAX, :]
        down = remote(edge.at[0], halo.at[1], h_send.at[2 * n], h_recv.at[2 * n], beside(-1))
        up = remote(edge.at[1], halo.at[0], h_send.at[2 * n + 1], h_recv.at[2 * n + 1], beside(1))

        @pl.when(j > 0)
        def _():
            down.start()

        @pl.when(j < 7)
        def _():
            up.start()

        def finish():
            @pl.when(j > 0)
            def _():
                up.wait_recv()
                pad[..., 0:DMAX, :] = halo[0]
                down.wait_send()

            @pl.when(j == 0)
            def _():
                pad[..., 0:DMAX, :] = jnp.zeros(lead + (DMAX, width), BF16)

            @pl.when(j < 7)
            def _():
                down.wait_recv()
                pad[..., rows + DMAX : rows + 2 * DMAX, :] = halo[1]
                up.wait_send()

            @pl.when(j == 7)
            def _():
                pad[..., rows + DMAX : rows + 2 * DMAX, :] = jnp.zeros(lead + (DMAX, width), BF16)

        return finish

    both = jnp.zeros((2 * rows, x_ref.shape[1]), F32)
    for h in range(HEADS):
        both = both + dot(
            att_ref[h].reshape(2 * rows, VAL), w_out_ref[h * VAL : (h + 1) * VAL, :], ((1,), (0,))
        )
    mixed_ref[...] = x_ref[...].astype(F32) + both[:rows]
    tan_ref[...] = both[rows:]
    ends = jnp.where((j == 0) | (j == 7), 1, 2)
    pl.semaphore_wait(barrier, 11 + ends)
    features = x_ref.shape[1]
    width = conv_ref.shape[3]
    for layer in range(2):
        dilation = dil_ref[layer]
        act, slope = gelu_pair(mixed_ref[...])
        slope_ref[layer] = slope
        pad_ref[0, DMAX : DMAX + rows, :] = act.astype(BF16)
        pad_ref[1, DMAX : DMAX + rows, :] = (slope * tan_ref[...]).astype(BF16)
        finish = swap(layer, edge_ref.at[layer], halo_ref.at[layer], pad_ref, features)

        inner = dot(
            pad_ref[:, DMAX : DMAX + rows, :].reshape(2 * rows, features), conv_ref[layer, 1], ((1,), (0,))
        )
        finish()
        pick = picker(dilation, rows)
        value = dot(pick, pad_ref[0], ((1,), (0,))).astype(BF16)
        tangent = dot(pick, pad_ref[1], ((1,), (0,))).astype(BF16)
        for n, tap in ((0, 0), (1, 2)):
            window = jnp.concatenate([value[n * rows : (n + 1) * rows], tangent[n * rows : (n + 1) * rows]], axis=0)
            inner = inner + dot(window, conv_ref[layer, tap], ((1,), (0,)))
        hidden, hslope = gelu_pair(inner[:rows])
        hslope_ref[layer] = hslope
        hidden = jnp.concatenate([hidden, hslope * inner[rows:]], axis=0).astype(BF16)
        point = dot(hidden, point_ref[layer], ((1,), (0,)))
        if layer == 0:
            mixed_ref[...] += point[:rows]
        tan_ref[...] += point[rows:]
    out_ref[...] = tan_ref[...].astype(BF16)
    sends = []
    for k in range(4):
        sends.append(
            remote(
                out_ref.at[pl.ds(64 * k, 64)], tan_out_ref.at[owners.slot], o_send.at[k], o_recv.at[owners.slot], owners.dst(k)
            )
        )
        sends[-1].start()
    grad_out_ref[...] = curve_ref[...] * tan_ref[...]
    for layer in (1, 0):
        dilation = dil_ref[layer]
        back = dot(grad_out_ref[...].astype(BF16), point_ref[layer], ((1,), (1,)))
        gpad_ref[DMAX : DMAX + rows, :] = (back * hslope_ref[layer]).astype(BF16)
        finish = swap(2 + layer, gedge_ref.at[layer], ghalo_ref.at[layer], gpad_ref, width)

        act = dot(gpad_ref[DMAX : DMAX + rows, :], conv_ref[layer, 1], ((1,), (1,)))
        finish()
        windows = dot(picker(dilation, rows), gpad_ref[...], ((1,), (0,))).astype(BF16)
        act = act + dot(windows[:rows], conv_ref[layer, 2], ((1,), (1,)))
        act = act + dot(windows[rows:], conv_ref[layer, 0], ((1,), (1,)))
        grad_out_ref[...] += slope_ref[layer] * act
    final = grad_out_ref[...].astype(BF16)
    for h in range(HEADS):
        ga_ref[h] = dot(final, w_out_ref[h * VAL : (h + 1) * VAL, :], ((1,), (1,))).astype(BF16)

    def start(k, carry):
        i = (j + k) % 8
        remote(ga_ref.at[i], item_ref.at[j], g_send.at[i], g_recv.at[j], group.dst(i)).start()
        return carry

    lax.fori_loop(1, 8, start, 0)
    own = pltpu.make_async_copy(ga_ref.at[j], item_ref.at[j], g_send.at[j])
    own.start()
    own.wait()

    def end(k, carry):
        i = (j + k) % 8
        remote(ga_ref.at[i], item_ref.at[i], g_send.at[i], g_recv.at[i], group.dst(i)).wait()
        return carry

    lax.fori_loop(1, 8, end, 0)
    for k in range(4):
        sends[k].wait_send()
        remote(out_ref.at[pl.ds(64 * k, 64)], tan_out_ref.at[k], o_send.at[k], o_recv.at[k], owners.dst(k)).wait_recv()


def conv_chain(dilations, attended, x_home, curve, w_out, conv_weight, point_weight, collective_id):
    rows, features = x_home.shape
    width = conv_weight.shape[3]
    vmem = pl.BlockSpec(memory_space=pltpu.VMEM)
    anywhere = pl.BlockSpec(memory_space=pl.ANY)
    return pl.pallas_call(
        conv_kernel,
        out_shape=[
            jax.ShapeDtypeStruct((4, 64, features), BF16),
            jax.ShapeDtypeStruct((rows, features), F32),
            jax.ShapeDtypeStruct((8, rows, VAL), BF16),
        ],
        in_specs=[pl.BlockSpec(memory_space=pltpu.SMEM)] + [vmem] * 6,
        out_specs=[anywhere, vmem, anywhere],
        scratch_shapes=[
            pltpu.VMEM((rows, features), F32),
            pltpu.VMEM((rows, features), F32),
            pltpu.VMEM((2, rows, features), F32),
            pltpu.VMEM((2, rows, width), F32),
            pltpu.VMEM((2, rows + 2 * DMAX, features), BF16),
            pltpu.VMEM((rows + 2 * DMAX, width), BF16),
            pltpu.VMEM((2, 2, 2, DMAX, features), BF16),
            pltpu.VMEM((2, 2, 2, DMAX, features), BF16),
            pltpu.VMEM((2, 2, DMAX, width), BF16),
            pltpu.VMEM((2, 2, DMAX, width), BF16),
            pltpu.VMEM((rows, features), BF16),
            pltpu.VMEM((8, rows, VAL), BF16),
            pltpu.SemaphoreType.DMA((8,)),
            pltpu.SemaphoreType.DMA((8,)),
            pltpu.SemaphoreType.DMA((4,)),
            pltpu.SemaphoreType.DMA((4,)),
            pltpu.SemaphoreType.DMA((8,)),
            pltpu.SemaphoreType.DMA((8,)),
        ],
        compiler_params=pltpu.CompilerParams(
            collective_id=collective_id, has_side_effects=True, vmem_limit_bytes=VMEM_LIMIT
        ),
    )(dilations, attended, x_home, curve, w_out, conv_weight, point_weight)


def back_kernel(
    qt_ref, kt_ref, v_ref, g_ref, lse_ref, att_ref, normed_ref,
    x_ref, grad_ref, gain_ref, wq_ref, wk_ref, wv_ref,
    out_c_ref, gvq_ref, gvk_ref,
    q_ref, kT_ref, delta_ref, acc_ref, pairT_ref,
    dv_buf, dv_ref, pair_buf, pair_ref, part_buf, part_ref,
    buf_ref, rows_ref, got_ref,
    v_send, v_recv, p_send, p_recv, e_send, e_recv, o_send, o_recv, r_send, r_recv,
):
    ctx, head = me()
    j = chunk_of(ctx, head)
    scale = KEY**-0.5
    owners = owner_stream()
    rows = rows_stream()
    plane = plane_stream()
    barrier = pltpu.get_barrier_semaphore()
    for d in range(1, 8):
        signal(barrier, member(ctx, head, (j + d) % 8))
    for k in range(4):
        signal(barrier, owners.src(k))
    for k in range(8):
        signal(barrier, rows.src(k))

    def greet(d, carry):
        signal(barrier, plane.src((plane.own + d) % 32))
        return carry

    lax.fori_loop(1, 32, greet, 0)
    for c in range(8):
        at = slice(c * BLOCK, (c + 1) * BLOCK)
        prod = g_ref[at, :].astype(F32) * att_ref[at, :VAL]
        prod = jnp.concatenate([prod, jnp.zeros((BLOCK, 128 - VAL), F32)], axis=1)
        delta_ref[:, at] = jnp.broadcast_to(jnp.sum(prod.T, axis=0, keepdims=True), (8, BLOCK))
        kT_ref[:, at] = kt_ref[at, :].astype(F32).T[:KEY].astype(BF16)
    q_ref[...] = qt_ref[:, KEY:]
    acc_ref[...] = jnp.zeros(acc_ref.shape, F32)
    pl.semaphore_wait(barrier, 50)

    def block(t, carry):
        i = (j + 1 + t) % 8
        at = pl.ds(pl.multiple_of(i * BLOCK, BLOCK), BLOCK)
        s = dot(kt_ref[at, :KEY], q_ref[...], ((1,), (1,))) * scale
        w = jnp.exp(s - lse_ref[0:1, :])
        dp = dot(v_ref[at, :VAL], g_ref[...], ((1,), (1,)))
        ds = (w * (dp - delta_ref[0:1, :]) * scale).astype(BF16)
        dv = dot(w.astype(BF16), g_ref[...], ((1,), (0,))).astype(BF16)

        @pl.when(t < 7)
        def _():
            dv_buf[i] = dv
            remote(dv_buf.at[i], dv_ref.at[j], v_send.at[i], v_recv.at[j], member(ctx, head, i)).start()

        @pl.when(t == 7)
        def _():
            dv_ref[j] = dv

        dk = dot(ds, q_ref[...], ((1,), (0,)))
        dk = jnp.concatenate([jnp.zeros((BLOCK, KEY), F32), dk], axis=1)
        pairT_ref[KEY:, at] = dk.T[KEY:].astype(BF16)
        acc_ref[...] += dot(kT_ref[:, at], ds, ((1,), (0,)))
        return carry

    lax.fori_loop(0, 8, block, 0)
    pairT_ref[:KEY, :] = acc_ref[...].astype(BF16)

    def pair_out(t, carry):
        i = (j + 1 + t) % 8
        at = pl.ds(pl.multiple_of(i * BLOCK, BLOCK), BLOCK)
        pair = pairT_ref[:, at].astype(F32).T.astype(BF16)

        @pl.when(t < 7)
        def _():
            pair_buf[i] = pair
            remote(pair_buf.at[i], pair_ref.at[j], p_send.at[i], p_recv.at[j], member(ctx, head, i)).start()

        @pl.when(t == 7)
        def _():
            pair_ref[j] = pair

        return carry

    lax.fori_loop(0, 8, pair_out, 0)
    part = dot(pairT_ref[...], normed_ref[...], ((1,), (0,)))
    part_buf[...] = part.T.reshape(part_buf.shape)
    part_ref[plane.own] = part_buf[plane.own]

    def part_out(d, carry):
        k = (plane.own + d) % 32
        remote(part_buf.at[k], part_ref.at[plane.slot], e_send.at[k], e_recv.at[plane.slot], plane.dst(k)).start()
        return carry

    lax.fori_loop(1, 32, part_out, 0)

    def group_end(t, carry):
        i = (j + 1 + t) % 8
        remote(dv_buf.at[i], dv_ref.at[i], v_send.at[i], v_recv.at[i], member(ctx, head, i)).wait()
        remote(pair_buf.at[i], pair_ref.at[i], p_send.at[i], p_recv.at[i], member(ctx, head, i)).wait()
        return carry

    lax.fori_loop(0, 7, group_end, 0)
    inputs = x_ref[...].astype(F32)
    count, features = inputs.shape
    acc = jnp.zeros((count, features), F32)
    for h in range(HEADS):
        w = jnp.concatenate([wq_ref[:, h * KEY : (h + 1) * KEY], wk_ref[:, h * KEY : (h + 1) * KEY]], axis=1)
        acc = acc + dot(pair_ref[h], w, ((1,), (1,)))
        acc = acc + dot(dv_ref[h], wv_ref[:, h * VAL : (h + 1) * VAL], ((1,), (1,)))
    gained = acc * gain_ref[...]
    spread = jnp.sqrt(jnp.mean(inputs * inputs, axis=-1, keepdims=True) + 1e-06)
    along = jnp.sum(gained * inputs, axis=-1, keepdims=True)
    inv = 1.0 / spread
    buf_ref[...] = (
        grad_ref[...] + gained * inv - inputs * (along / (features * spread * spread * spread))
    ).astype(BF16)
    for k in range(4):
        remote(
            buf_ref.at[pl.ds(64 * k, 64)], out_c_ref.at[owners.slot], o_send.at[k], o_recv.at[owners.slot], owners.dst(k)
        ).start()

    def part_end(d, carry):
        k = (plane.own + d) % 32
        remote(part_buf.at[k], part_ref.at[k], e_send.at[k], e_recv.at[k], plane.dst(k)).wait()
        return carry

    lax.fori_loop(1, 32, part_end, 0)
    summed = jnp.sum(part_ref[...], axis=0) * (1.0 / (32.0 * 2048.0))
    for k in range(8):
        rows_ref[k, 0:3, :] = summed[3 * k : 3 * k + 3, :]
        rows_ref[k, 3:8, :] = jnp.zeros((5, 2 * KEY), F32)
    for k in range(8):
        remote(rows_ref.at[k], got_ref.at[rows.slot], r_send.at[k], r_recv.at[rows.slot], rows.dst(k)).start()
    for k in range(8):
        remote(rows_ref.at[k], got_ref.at[k], r_send.at[k], r_recv.at[k], rows.dst(k)).wait()
    for k in range(8):
        gvq_ref[:, k * KEY : (k + 1) * KEY] = got_ref[k, 0:3, :KEY]
        gvk_ref[:, k * KEY : (k + 1) * KEY] = got_ref[k, 0:3, KEY:]
    for k in range(4):
        remote(
            buf_ref.at[pl.ds(64 * k, 64)], out_c_ref.at[k], o_send.at[k], o_recv.at[k], owners.dst(k)
        ).wait()


def back(qt, kt, v, grad_item, lse, att, normed_all, x_home, gradient, gain, wq, wk, wv, collective_id):
    rows, features = x_home.shape
    length = qt.shape[0]
    vmem = pl.BlockSpec(memory_space=pltpu.VMEM)
    dma = pltpu.SemaphoreType.DMA
    return pl.pallas_call(
        back_kernel,
        out_shape=[
            jax.ShapeDtypeStruct((4, 64, features), BF16),
            jax.ShapeDtypeStruct((3, HEADS * KEY), F32),
            jax.ShapeDtypeStruct((3, HEADS * KEY), F32),
        ],
        in_specs=[vmem] * 13,
        out_specs=[pl.BlockSpec(memory_space=pl.ANY), vmem, vmem],
        scratch_shapes=[
            pltpu.VMEM((length, KEY), BF16),
            pltpu.VMEM((KEY, length), BF16),
            pltpu.VMEM((8, length), F32),
            pltpu.VMEM((KEY, length), F32),
            pltpu.VMEM((2 * KEY, length), BF16),
            pltpu.VMEM((8, rows, VAL), BF16),
            pltpu.VMEM((8, rows, VAL), BF16),
            pltpu.VMEM((8, rows, 2 * KEY), BF16),
            pltpu.VMEM((8, rows, 2 * KEY), BF16),
            pltpu.VMEM((32, features // 32, 2 * KEY), F32),
            pltpu.VMEM((32, features // 32, 2 * KEY), F32),
            pltpu.VMEM((rows, features), BF16),
            pltpu.VMEM((8, 8, 2 * KEY), F32),
            pltpu.VMEM((8, 8, 2 * KEY), F32),
            dma((8,)),
            dma((8,)),
            dma((8,)),
            dma((8,)),
            dma((32,)),
            dma((32,)),
            dma((4,)),
            dma((4,)),
            dma((8,)),
            dma((8,)),
        ],
        compiler_params=pltpu.CompilerParams(
            collective_id=collective_id, has_side_effects=True, vmem_limit_bytes=VMEM_LIMIT
        ),
    )(qt, kt, v, grad_item, lse, att, normed_all, x_home, gradient, gain, wq, wk, wv)


def per_device(
    window_input,
    norm_gain,
    w_query,
    w_key,
    w_value,
    w_out,
    conv_weight,
    point_weight,
    dilations,
    tangent_query,
    tangent_key,
    curvature,
):
    features = window_input.shape[2]
    curves = jnp.pad(curvature[:, None, :], ((0, 0), (0, 7), (0, 64)))
    gain = norm_gain[None, :]
    x_home, c_home, normed_all, qt, kt, v = front(
        window_input, curves, gain, w_query, tangent_query, w_key, tangent_key, w_value, 0
    )
    x_home = x_home.reshape(256, features)
    curve = c_home[:, 0, :64].reshape(256, 1)
    attended, lse, att = attend_forward(qt, kt, v, 1)
    out_t, gradient, grad_item = conv_chain(
        dilations, attended, x_home, curve, w_out, conv_weight, point_weight, 2
    )
    out_c, gv_query, gv_key = back(
        qt,
        kt,
        v,
        grad_item.reshape(2048, VAL),
        lse,
        att,
        normed_all.reshape(2048, features),
        x_home,
        gradient,
        gain,
        w_query,
        w_key,
        w_value,
        3,
    )
    return out_t, out_c, gv_query, gv_key


def solution(mesh):
    in_specs = (P("head", "ctx", None),) + (P(),) * 10 + (P("head", "ctx"),)
    out_specs = (
        P("head", "ctx", None),
        P("head", "ctx", None),
        P(("ctx", "head"), None),
        P(("ctx", "head"), None),
    )
    return jax.shard_map(per_device, mesh=mesh, in_specs=in_specs, out_specs=out_specs, check_vma=False)
```

```python
import functools

import jax
import jax.numpy as jnp
from jax import lax
from jax.experimental import pallas as pl
from jax.experimental.pallas import tpu as pltpu
from jax.sharding import PartitionSpec as P

HEADS = 8
KEY = 64
VAL = 96
DMAX = 16
MESH = pl.DeviceIdType.MESH
VMEM_LIMIT = 56 * 2**20
F32 = jnp.float32
BF16 = jnp.bfloat16
BLOCK = 256
SCALE = KEY**-0.5


def place(ctx, head):
    return ctx // 8, (ctx // 4) % 2 * 4 + head // 2, ctx % 4, head % 2


def device(y, z, x, core):
    return y * 8 + z // 4 * 4 + x, z % 4 * 2 + core


def chunk_of(ctx, head):
    return ctx // 8 * 2 + head % 2


def member(ctx, head, j):
    _, z, x, _ = place(ctx, head)
    return device(j // 2, z, x, j % 2)


def home_of(ctx, head, b):
    y, z, _, core = place(ctx, head)
    return device(y, core * 4 + (z % 4 + 2) % 4, b, z // 4)


def owner_of(ctx, head, x0):
    y, z, _, core = place(ctx, head)
    return device(y, core * 4 + (z % 4 + 2) % 4, x0, z // 4)


def me():
    return lax.axis_index("ctx"), lax.axis_index("head")


def signal(barrier, target):
    pl.semaphore_signal(barrier, inc=1, device_id=target, device_id_type=MESH)


def remote(src, dst, send, recv, target):
    return pltpu.make_async_remote_copy(
        src_ref=src, dst_ref=dst, send_sem=send, recv_sem=recv, device_id=target, device_id_type=MESH
    )


class Stream:
    def __init__(self, count, dst, src, slot, own):
        self.count, self.dst, self.src, self.slot, self.own = count, dst, src, slot, own


def home_stream():
    ctx, head = me()
    return Stream(4, lambda i: home_of(ctx, head, i), lambda k: owner_of(ctx, head, k), ctx % 4, None)


def owner_stream():
    ctx, head = me()
    return Stream(4, lambda i: owner_of(ctx, head, i), lambda k: home_of(ctx, head, k), ctx % 4, None)


def group_stream():
    ctx, head = me()
    return Stream(
        8, lambda i: member(ctx, head, i), lambda k: member(ctx, head, k), chunk_of(ctx, head), chunk_of(ctx, head)
    )


def plane_stream():
    ctx, head = me()
    y, z, x, core = place(ctx, head)

    def at(r):
        return device(y, r // 4 % 2 * 4 + r // 8, (r + 3) % 4, core)

    rank = z % 4 * 8 + z // 4 * 4 + (x + 1) % 4
    return Stream(32, at, at, rank, rank)


def rows_stream():
    ctx, head = me()
    _, z, x, _ = place(ctx, head)
    r = z % 4 * 8 + z // 4 * 4 + (x + 1) % 4

    def src(k):
        return device(k // 2, ctx // 4 % 2 * 4 + ctx // 8, (ctx + 3) % 4, k % 2)

    return Stream(8, lambda i: (r, i), src, chunk_of(ctx, head), None)


def dot(a, b, contract):
    return lax.dot_general(a, b, ((contract[0], contract[1]), ((), ())), preferred_element_type=F32)


class Refs:
    def __init__(self, names, refs):
        for name, ref in zip(names, refs, strict=True):
            setattr(self, name, ref)


def greet_all(r, barrier):
    ctx, head = me()
    j = chunk_of(ctx, head)
    homes, owners, rows, plane = home_stream(), owner_stream(), rows_stream(), plane_stream()
    for k in range(4):
        signal(barrier, homes.src(k))
        signal(barrier, owners.src(k))
    for d in range(1, 8):
        signal(barrier, member(ctx, head, (j + d) % 8))
    for k in range(8):
        signal(barrier, rows.src(k))

    def greet(d, carry):
        signal(barrier, plane.src((plane.own + d) % 32))
        return carry

    lax.fori_loop(1, 32, greet, 0)


def front(r):
    ctx, head = me()
    j = chunk_of(ctx, head)
    core = j % 2
    homes = home_stream()
    sibling = j + 1 - 2 * core
    up, down, far = (j + 2) % 8, (j + 6) % 8, (j + 4) % 8
    for k in range(4):
        remote(r.x.at[k], r.home.at[homes.slot], r.x_send.at[k], r.x_recv.at[homes.slot], homes.dst(k)).start()
    for k in range(4):
        r.c_buf[k] = jnp.zeros((8, 128), F32)
        r.c_buf[k, 0:1, 0:64] = r.curvature[k : k + 1, :]
        remote(r.c_buf.at[k], r.c_home.at[homes.slot], r.c_send.at[k], r.c_recv.at[homes.slot], homes.dst(k)).start()

    def columns(weight, size, at, factor):
        shape = (weight.shape[1], 384)
        row = lax.broadcasted_iota(jnp.int32, shape, 0)
        column = lax.broadcasted_iota(jnp.int32, shape, 1)
        hit = (row - j * size == column - at) & (column >= at) & (column < at + size)
        return dot(weight[...], jnp.where(hit, factor, 0.0).astype(BF16), ((1,), (0,)))

    joined = None
    for name, size, at, factor in (
        ("tq", KEY, 0, SCALE),
        ("wq", KEY, KEY, SCALE),
        ("wk", KEY, 2 * KEY, 1.0),
        ("tk", KEY, 3 * KEY, 1.0),
        ("wv", VAL, 4 * KEY, 1.0),
    ):
        fetch(r, name).wait()
        part = columns(getattr(r, name), size, at, factor)
        joined = part if joined is None else joined + part
    r.joined[...] = joined.astype(BF16)

    def piece(i, p):
        return r.normed.at[i, pl.ds(64 * p, 64)]

    def push(i, p, way, to):
        remote(piece(i, p), piece(i, p), r.n_send.at[i, p, way], r.n_recv.at[i, p], member(ctx, head, to)).start()

    def arrived(i, p):
        remote(
            piece(i, p), piece(i, p), r.n_send.at[i, p, 0], r.n_recv.at[i, p], member(ctx, head, sibling)
        ).wait_recv()

    def sent(i, p, way, to):
        remote(piece(i, p), piece(i, p), r.n_send.at[i, p, way], r.n_recv.at[i, p], member(ctx, head, to)).wait_send()

    gain = r.gain[...].reshape(1, -1)
    for p in range(4):
        remote(r.x.at[p], r.home.at[p], r.x_send.at[p], r.x_recv.at[p], homes.dst(p)).wait_recv()
        inputs = r.home[p].astype(F32)
        spread = jnp.sqrt(jnp.mean(inputs * inputs, axis=-1, keepdims=True) + 1e-06)
        r.normed[j, 64 * p : 64 * p + 64, :] = (inputs / spread * gain).astype(BF16)
        push(j, p, 1, up)
        push(j, p, 2, down)
        push(j, p, 0, sibling)

    def project(i):
        rows = pl.ds(pl.multiple_of(i * BLOCK, BLOCK), BLOCK)
        proj = dot(r.normed[i], r.joined[...], ((1,), (0,))).astype(BF16)
        r.qt[rows, :] = proj[:, :128]
        r.kt[rows, :] = proj[:, 128:256]
        lane = lax.broadcasted_iota(jnp.int32, (BLOCK, 128), 1)
        r.v[rows, :] = jnp.where(lane < VAL, proj[:, 256:].astype(F32), 1.0).astype(BF16)

    for p in range(4):
        arrived(down, p)
        if p < 2:
            push(down, p, 1, up)
        push(down, p, 0, sibling)
        arrived(up, p)
        if p >= 2:
            push(up, p, 2, down)
        push(up, p, 0, sibling)
    project(j)
    project(down)
    project(up)
    for p in (0, 2, 1, 3):
        arrived(far, p)
        push(far, p, 0, sibling)
    project(far)
    for d in (0, 2, 6, 4):
        i = (sibling + d) % 8
        for p in range(4):
            arrived(i, p)
        project(i)
    for k in range(4):
        remote(r.x.at[k], r.home.at[k], r.x_send.at[k], r.x_recv.at[k], homes.dst(k)).wait_send()
        remote(r.c_buf.at[k], r.c_home.at[k], r.c_send.at[k], r.c_recv.at[k], homes.dst(k)).wait()
    for p in range(4):
        sent(j, p, 1, up)
        sent(j, p, 2, down)
        for i in (j, up, down, far):
            sent(i, p, 0, sibling)
        if p < 2:
            sent(down, p, 1, up)
        else:
            sent(up, p, 2, down)


def attend_forward(r):
    ctx, head = me()
    j = chunk_of(ctx, head)

    def block(t, carry):
        i = (j + 1 + t) % 8
        rows = pl.ds(pl.multiple_of(i * BLOCK, BLOCK), BLOCK)
        qt = r.qt[rows, :]
        s = dot(qt[:, KEY:], r.kt[:, :KEY], ((1,), (1,)))
        top = jnp.max(s, axis=1, keepdims=True)
        p = jnp.exp(s - top)
        ext = dot(p.astype(BF16), r.v[...], ((1,), (0,)))
        total = ext[:, VAL : VAL + 1]
        inv = 1.0 / total
        ts = dot(qt, r.kt[...], ((1,), (1,)))
        mean = jnp.sum(p * ts, axis=1, keepdims=True) / jnp.sum(p, axis=1, keepdims=True)
        tw = p * (ts - mean)
        tan = dot(tw.astype(BF16), r.v[...], ((1,), (0,))) * inv
        att = ext * inv

        @pl.when(t < 7)
        def _():
            r.att_buf[i, 0] = att[:, :VAL].astype(BF16)
            r.att_buf[i, 1] = tan[:, :VAL].astype(BF16)
            remote(
                r.att_buf.at[i], r.attended.at[j], r.a_send.at[i], r.a_recv.at[j], member(ctx, head, i)
            ).start()

        @pl.when(t == 7)
        def _():
            r.attended[j, 0] = att[:, :VAL].astype(BF16)
            r.attended[j, 1] = tan[:, :VAL].astype(BF16)

        r.att[rows, :] = att
        r.lse[:, rows] = jnp.broadcast_to(top + jnp.log(total), (BLOCK, 128)).T[:8]
        return carry

    lax.fori_loop(0, 8, block, 0)

    def end(t, carry):
        i = (j + 1 + t) % 8
        remote(r.att_buf.at[i], r.attended.at[i], r.a_send.at[i], r.a_recv.at[i], member(ctx, head, i)).wait()
        return carry

    lax.fori_loop(0, 7, end, 0)


def gelu_pair(v):
    root = 0.7978845608028654
    square = v * v
    t = jnp.tanh(root * (v + 0.044715 * v * square))
    half = 0.5 * (1.0 + t)
    return v * half, half + 0.5 * v * (1.0 - t * t) * (root + (3.0 * 0.044715 * root) * square)


def picker(dilation, rows):
    shape = (2 * rows, rows + 2 * DMAX)
    row = lax.broadcasted_iota(jnp.int32, shape, 0)
    column = lax.broadcasted_iota(jnp.int32, shape, 1)
    wanted = jnp.where(row < rows, row + DMAX - dilation, row - rows + DMAX + dilation)
    return jnp.where(column == wanted, 1.0, 0.0).astype(BF16)


def conv_chain(r):
    ctx, head = me()
    j = chunk_of(ctx, head)
    rows, features, width = BLOCK, r.w_out.shape[1], r.conv.shape[3]
    owners = owner_stream()

    def beside(step):
        return member(ctx, head, (j + step + 8) % 8)

    def swap(n, edge, halo, pad, width):
        lead = pad.shape[:-2]
        edge[0] = pad[..., DMAX : 2 * DMAX, :]
        edge[1] = pad[..., rows : rows + DMAX, :]
        down = remote(edge.at[0], halo.at[1], r.h_send.at[2 * n], r.h_recv.at[2 * n], beside(-1))
        up = remote(edge.at[1], halo.at[0], r.h_send.at[2 * n + 1], r.h_recv.at[2 * n + 1], beside(1))

        @pl.when(j > 0)
        def _():
            down.start()

        @pl.when(j < 7)
        def _():
            up.start()

        def finish():
            @pl.when(j > 0)
            def _():
                up.wait_recv()
                pad[..., 0:DMAX, :] = halo[0]
                down.wait_send()

            @pl.when(j == 0)
            def _():
                pad[..., 0:DMAX, :] = jnp.zeros(lead + (DMAX, width), BF16)

            @pl.when(j < 7)
            def _():
                down.wait_recv()
                pad[..., rows + DMAX : rows + 2 * DMAX, :] = halo[1]
                up.wait_send()

            @pl.when(j == 7)
            def _():
                pad[..., rows + DMAX : rows + 2 * DMAX, :] = jnp.zeros(lead + (DMAX, width), BF16)

        return finish

    for name in ("w_out", "conv", "point"):
        fetch(r, name).wait()
    both = jnp.zeros((2 * rows, features), F32)
    for h in range(HEADS):
        both = both + dot(r.attended[h].reshape(2 * rows, VAL), r.w_out[h * VAL : (h + 1) * VAL, :], ((1,), (0,)))
    r.mixed[...] = r.home[...].reshape(rows, features).astype(F32) + both[:rows]
    r.tan[...] = both[rows:]
    for layer in range(2):
        dilation = r.dilations[layer]
        act, slope = gelu_pair(r.mixed[...])
        r.slope[layer] = slope
        r.pad[0, DMAX : DMAX + rows, :] = act.astype(BF16)
        r.pad[1, DMAX : DMAX + rows, :] = (slope * r.tan[...]).astype(BF16)
        finish = swap(layer, r.edge.at[layer], r.halo.at[layer], r.pad, features)
        inner = dot(r.pad[:, DMAX : DMAX + rows, :].reshape(2 * rows, features), r.conv[layer, 1], ((1,), (0,)))
        pick = picker(dilation, rows)
        finish()
        value = dot(pick, r.pad[0], ((1,), (0,))).astype(BF16)
        tangent = dot(pick, r.pad[1], ((1,), (0,))).astype(BF16)
        for n, tap in ((0, 0), (1, 2)):
            window = jnp.concatenate([value[n * rows : (n + 1) * rows], tangent[n * rows : (n + 1) * rows]], axis=0)
            inner = inner + dot(window, r.conv[layer, tap], ((1,), (0,)))
        hidden, hslope = gelu_pair(inner[:rows])
        r.hslope[layer] = hslope
        hidden = jnp.concatenate([hidden, hslope * inner[rows:]], axis=0).astype(BF16)
        point = dot(hidden, r.point[layer], ((1,), (0,)))
        if layer == 0:
            r.mixed[...] += point[:rows]
        r.tan[...] += point[rows:]
    r.out_buf[0] = r.tan[...].astype(BF16)
    for k in range(4):
        out_copy(r, 0, k, owners.slot, owners.dst(k)).start()
    for k in range(4):
        curve = r.c_home[k].T[:64, 0:1]
        at = slice(64 * k, 64 * k + 64)
        r.grad[at, :] = curve * r.tan[at, :]
    for layer in (1, 0):
        dilation = r.dilations[layer]
        back = dot(r.grad[...].astype(BF16), r.point[layer], ((1,), (1,)))
        r.gpad[DMAX : DMAX + rows, :] = (back * r.hslope[layer]).astype(BF16)
        finish = swap(2 + layer, r.gedge.at[layer], r.ghalo.at[layer], r.gpad, width)
        act = dot(r.gpad[DMAX : DMAX + rows, :], r.conv[layer, 1], ((1,), (1,)))
        pick = picker(dilation, rows)
        finish()
        windows = dot(pick, r.gpad[...], ((1,), (0,))).astype(BF16)
        act = act + dot(windows[:rows], r.conv[layer, 2], ((1,), (1,)))
        act = act + dot(windows[rows:], r.conv[layer, 0], ((1,), (1,)))
        r.grad[...] += r.slope[layer] * act
    final = r.grad[...].astype(BF16)

    def send(t, carry):
        i = (j + 1 + t) % 8
        part = r.w_out[pl.ds(pl.multiple_of(i * VAL, 32), VAL), :]
        ga = dot(final, part, ((1,), (1,))).astype(BF16)

        @pl.when(t < 7)
        def _():
            r.ga_buf[i] = ga
            remote(r.ga_buf.at[i], r.item.at[j], r.g_send.at[i], r.g_recv.at[j], member(ctx, head, i)).start()

        @pl.when(t == 7)
        def _():
            r.item[j] = ga

        return carry

    lax.fori_loop(0, 8, send, 0)


def out_copy(r, n, k, slot, target):
    out = (r.out_t, r.out_c)[n]
    return remote(
        r.out_buf.at[n, pl.ds(64 * k, 64)], out.at[slot], r.o_send.at[n, k], r.o_recv.at[n, slot], target
    )


def back(r):
    ctx, head = me()
    j = chunk_of(ctx, head)
    owners, rows, plane = owner_stream(), rows_stream(), plane_stream()
    length = 8 * BLOCK
    r.q[...] = r.qt[:, KEY:]
    r.acc[...] = jnp.zeros(r.acc.shape, F32)
    for c in range(8):
        at = slice(c * BLOCK, (c + 1) * BLOCK)
        r.kT[:, at] = (r.kt[at, :].astype(F32).T[:KEY] * SCALE).astype(BF16)

    def ga_end(t, carry):
        i = (j + 1 + t) % 8
        remote(r.ga_buf.at[i], r.item.at[i], r.g_send.at[i], r.g_recv.at[i], member(ctx, head, i)).wait()
        return carry

    lax.fori_loop(0, 7, ga_end, 0)
    for c in range(8):
        at = slice(c * BLOCK, (c + 1) * BLOCK)
        prod = r.item[c].astype(F32) * r.att[at, :VAL]
        prod = jnp.concatenate([prod, jnp.zeros((BLOCK, 128 - VAL), F32)], axis=1)
        r.delta[:, at] = jnp.broadcast_to(jnp.sum(prod.T, axis=0, keepdims=True), (8, BLOCK))

    def packed(a):
        return jnp.concatenate([a[: BLOCK // 2], a[BLOCK // 2 :]], axis=1)

    def deliver(buf, ref, send, recv, i, t, value):
        @pl.when(t < 7)
        def _():
            buf[i] = value
            remote(buf.at[i], ref.at[j], send.at[i], recv.at[j], member(ctx, head, i)).start()

        @pl.when(t == 7)
        def _():
            ref[j] = value

    def block(t, carry):
        i = (j + 1 + t) % 8
        at = pl.ds(pl.multiple_of(i * BLOCK, BLOCK), BLOCK)
        g = r.item[...].reshape(length, VAL)
        s = dot(r.kt[at, :KEY], r.q[...], ((1,), (1,)))
        w = jnp.exp(s - r.lse[0:1, :])
        dp = dot(r.v[at, :VAL], g, ((1,), (1,)))
        ds = (w * (dp - r.delta[0:1, :])).astype(BF16)
        dv = dot(w.astype(BF16), g, ((1,), (0,))).astype(BF16)
        deliver(r.dv_buf, r.dv, r.v_send, r.v_recv, i, t, dv)
        dk = packed(dot(ds, r.q[...], ((1,), (0,))))
        deliver(r.dk_buf, r.dk, r.k_send, r.k_recv, i, t, dk.astype(BF16))
        dkT = dk.T
        r.pairT[KEY:, at] = jnp.concatenate([dkT[:KEY], dkT[KEY:]], axis=1).astype(BF16)
        r.acc[...] += dot(r.kT[:, at], ds, ((1,), (0,)))
        return carry

    lax.fori_loop(0, 8, block, 0)

    def dq_out(t, carry):
        i = (j + 1 + t) % 8
        at = pl.ds(pl.multiple_of(i * BLOCK, BLOCK), BLOCK)
        part = r.acc[:, at]
        dq = jnp.concatenate([part[:, : BLOCK // 2], part[:, BLOCK // 2 :]], axis=0).T.astype(BF16)
        deliver(r.dq_buf, r.dq, r.q_send, r.q_recv, i, t, dq)
        return carry

    lax.fori_loop(0, 8, dq_out, 0)
    r.pairT[:KEY, :] = r.acc[...].astype(BF16)
    part = dot(r.pairT[...], r.normed[...].reshape(length, -1), ((1,), (0,)))
    r.part_buf[...] = part.T.reshape(r.part_buf.shape)
    r.part[plane.own] = r.part_buf[plane.own]

    def part_out(d, carry):
        k = (plane.own + d) % 32
        remote(r.part_buf.at[k], r.part.at[plane.slot], r.e_send.at[k], r.e_recv.at[plane.slot], plane.dst(k)).start()
        return carry

    lax.fori_loop(1, 32, part_out, 0)

    def group_end(t, carry):
        i = (j + 1 + t) % 8
        to = member(ctx, head, i)
        remote(r.dv_buf.at[i], r.dv.at[i], r.v_send.at[i], r.v_recv.at[i], to).wait()
        remote(r.dk_buf.at[i], r.dk.at[i], r.k_send.at[i], r.k_recv.at[i], to).wait()
        remote(r.dq_buf.at[i], r.dq.at[i], r.q_send.at[i], r.q_recv.at[i], to).wait()
        return carry

    lax.fori_loop(0, 7, group_end, 0)
    inputs = r.home[...].reshape(BLOCK, -1).astype(F32)
    count, features = inputs.shape
    acc = jnp.zeros((count, features), F32)
    for h in range(HEADS):
        w = jnp.concatenate([r.wq[:, h * KEY : (h + 1) * KEY], r.wk[:, h * KEY : (h + 1) * KEY]], axis=1)
        dq, dk = r.dq[h], r.dk[h]
        pair = jnp.concatenate(
            [
                jnp.concatenate([dq[:, :KEY], dk[:, :KEY]], axis=1),
                jnp.concatenate([dq[:, KEY:], dk[:, KEY:]], axis=1),
            ],
            axis=0,
        )
        acc = acc + dot(pair, w, ((1,), (1,)))
        acc = acc + dot(r.dv[h], r.wv[:, h * VAL : (h + 1) * VAL], ((1,), (1,)))
    gained = acc * r.gain[...].reshape(1, -1)
    spread = jnp.sqrt(jnp.mean(inputs * inputs, axis=-1, keepdims=True) + 1e-06)
    along = jnp.sum(gained * inputs, axis=-1, keepdims=True)
    inv = 1.0 / spread
    r.out_buf[1] = (
        r.grad[...] + gained * inv - inputs * (along / (features * spread * spread * spread))
    ).astype(BF16)
    for k in range(4):
        out_copy(r, 1, k, owners.slot, owners.dst(k)).start()

    def part_end(d, carry):
        k = (plane.own + d) % 32
        remote(r.part_buf.at[k], r.part.at[k], r.e_send.at[k], r.e_recv.at[k], plane.dst(k)).wait()
        return carry

    lax.fori_loop(1, 32, part_end, 0)
    summed = jnp.sum(r.part[...], axis=0) * (1.0 / (32.0 * 2048.0))
    for k in range(8):
        r.rows[k, 0:3, :] = summed[3 * k : 3 * k + 3, :]
        r.rows[k, 3:8, :] = jnp.zeros((5, 2 * KEY), F32)
    for k in range(8):
        remote(r.rows.at[k], r.got.at[rows.slot], r.r_send.at[k], r.r_recv.at[rows.slot], rows.dst(k)).start()
    for k in range(8):
        remote(r.rows.at[k], r.got.at[k], r.r_send.at[k], r.r_recv.at[k], rows.dst(k)).wait()
    for k in range(8):
        r.gvq[:, k * KEY : (k + 1) * KEY] = r.got[k, 0:3, :KEY]
        r.gvk[:, k * KEY : (k + 1) * KEY] = r.got[k, 0:3, KEY:]
    for n in range(2):
        for k in range(4):
            out_copy(r, n, k, k, owners.dst(k)).wait()


WEIGHTS = ("tq", "wq", "wk", "tk", "wv", "w_out", "conv", "point")


def fetch(r, name):
    n = WEIGHTS.index(name)
    return pltpu.make_async_copy(getattr(r, name + "_hbm"), getattr(r, name), r.w_sem.at[n])


def whole_kernel(names, *refs):
    r = Refs(names, refs)
    barrier = pltpu.get_barrier_semaphore()
    greet_all(r, barrier)
    for name in WEIGHTS:
        fetch(r, name).start()
    pl.semaphore_wait(barrier, 54)
    front(r)
    attend_forward(r)
    conv_chain(r)
    back(r)


def run(inputs, collective_id):
    by_name = {name: array for name, array, _ in inputs}
    features = by_name["x"].shape[2]
    width = by_name["conv_hbm"].shape[3]
    length = 8 * BLOCK
    rows = BLOCK
    vmem, dma = pltpu.VMEM, pltpu.SemaphoreType.DMA
    scratch = {name: vmem(by_name[name + "_hbm"].shape, BF16) for name in WEIGHTS}
    scratch.update(
        w_sem=dma((len(WEIGHTS),)),
        home=vmem((4, 64, features), BF16),
        c_buf=vmem((4, 8, 128), F32),
        c_home=vmem((4, 8, 128), F32),
        joined=vmem((features, 384), BF16),
        normed=vmem((8, rows, features), BF16),
        qt=vmem((length, 128), BF16),
        kt=vmem((length, 128), BF16),
        v=vmem((length, 128), BF16),
        att_buf=vmem((8, 2, rows, VAL), BF16),
        attended=vmem((8, 2, rows, VAL), BF16),
        att=vmem((length, 128), F32),
        lse=vmem((8, length), F32),
        mixed=vmem((rows, features), F32),
        tan=vmem((rows, features), F32),
        grad=vmem((rows, features), F32),
        slope=vmem((2, rows, features), F32),
        hslope=vmem((2, rows, width), F32),
        pad=vmem((2, rows + 2 * DMAX, features), BF16),
        gpad=vmem((rows + 2 * DMAX, width), BF16),
        edge=vmem((2, 2, 2, DMAX, features), BF16),
        halo=vmem((2, 2, 2, DMAX, features), BF16),
        gedge=vmem((2, 2, DMAX, width), BF16),
        ghalo=vmem((2, 2, DMAX, width), BF16),
        out_buf=vmem((2, rows, features), BF16),
        ga_buf=vmem((8, rows, VAL), BF16),
        item=vmem((8, rows, VAL), BF16),
        q=vmem((length, KEY), BF16),
        kT=vmem((KEY, length), BF16),
        delta=vmem((8, length), F32),
        acc=vmem((KEY, length), F32),
        pairT=vmem((2 * KEY, length), BF16),
        dv_buf=vmem((8, rows, VAL), BF16),
        dv=vmem((8, rows, VAL), BF16),
        dk_buf=vmem((8, rows // 2, 2 * KEY), BF16),
        dk=vmem((8, rows // 2, 2 * KEY), BF16),
        dq_buf=vmem((8, rows // 2, 2 * KEY), BF16),
        dq=vmem((8, rows // 2, 2 * KEY), BF16),
        part_buf=vmem((32, features // 32, 2 * KEY), F32),
        part=vmem((32, features // 32, 2 * KEY), F32),
        rows=vmem((8, 8, 2 * KEY), F32),
        got=vmem((8, 8, 2 * KEY), F32),
    )
    for name, shape in (
        ("x", (4,)),
        ("c", (4,)),
        ("n", (8, 4)),
        ("a", (8,)),
        ("h", (8,)),
        ("o", (2, 4)),
        ("g", (8,)),
        ("v", (8,)),
        ("k", (8,)),
        ("q", (8,)),
        ("e", (32,)),
        ("r", (8,)),
    ):
        scratch[name + "_send"] = dma(shape + (3,)) if name == "n" else dma(shape)
        scratch[name + "_recv"] = dma(shape)
    outs = ("out_t", "out_c", "gvq", "gvk")
    names = [name for name, _, _ in inputs] + list(outs) + list(scratch)
    return pl.pallas_call(
        functools.partial(whole_kernel, names),
        out_shape=[
            jax.ShapeDtypeStruct((4, 64, features), BF16),
            jax.ShapeDtypeStruct((4, 64, features), BF16),
            jax.ShapeDtypeStruct((3, HEADS * KEY), F32),
            jax.ShapeDtypeStruct((3, HEADS * KEY), F32),
        ],
        in_specs=[pl.BlockSpec(memory_space=space) for _, _, space in inputs],
        out_specs=[pl.BlockSpec(memory_space=space) for space in (pl.ANY, pl.ANY, vmem, vmem)],
        scratch_shapes=list(scratch.values()),
        compiler_params=pltpu.CompilerParams(
            collective_id=collective_id, has_side_effects=True, vmem_limit_bytes=VMEM_LIMIT
        ),
    )(*[array for _, array, _ in inputs])


def per_device(
    window_input,
    norm_gain,
    w_query,
    w_key,
    w_value,
    w_out,
    conv_weight,
    point_weight,
    dilations,
    tangent_query,
    tangent_key,
    curvature,
):
    return run(
        (
            ("dilations", dilations, pltpu.SMEM),
            ("x", window_input, pl.ANY),
            ("curvature", curvature, pltpu.VMEM),
            ("gain", norm_gain, pltpu.VMEM),
            ("tq_hbm", tangent_query, pl.ANY),
            ("wq_hbm", w_query, pl.ANY),
            ("wk_hbm", w_key, pl.ANY),
            ("tk_hbm", tangent_key, pl.ANY),
            ("wv_hbm", w_value, pl.ANY),
            ("w_out_hbm", w_out, pl.ANY),
            ("conv_hbm", conv_weight, pl.ANY),
            ("point_hbm", point_weight, pl.ANY),
        ),
        0,
    )


def solution(mesh):
    in_specs = (P("head", "ctx", None),) + (P(),) * 10 + (P("head", "ctx"),)
    out_specs = (
        P("head", "ctx", None),
        P("head", "ctx", None),
        P(("ctx", "head"), None),
        P(("ctx", "head"), None),
    )
    return jax.shard_map(per_device, mesh=mesh, in_specs=in_specs, out_specs=out_specs, check_vma=False)
```

```python
import functools

import jax
import jax.numpy as jnp
from jax import lax
from jax.experimental import pallas as pl
from jax.experimental.pallas import tpu as pltpu
from jax.sharding import PartitionSpec as P

HEADS = 8
KEY = 64
VAL = 96
DMAX = 16
MESH = pl.DeviceIdType.MESH
VMEM_LIMIT = 56 * 2**20
F32 = jnp.float32
BF16 = jnp.bfloat16
BLOCK = 256
SCALE = KEY**-0.5


def place(ctx, head):
    return ctx // 8, (ctx // 4) % 2 * 4 + head // 2, ctx % 4, head % 2


def device(y, z, x, core):
    return y * 8 + z // 4 * 4 + x, z % 4 * 2 + core


def chunk_of(ctx, head):
    return ctx // 8 * 2 + head % 2


def member(ctx, head, j):
    _, z, x, _ = place(ctx, head)
    return device(j // 2, z, x, j % 2)


def home_of(ctx, head, b):
    y, z, _, core = place(ctx, head)
    return device(y, core * 4 + (z % 4 + 2) % 4, b, z // 4)


def owner_of(ctx, head, x0):
    y, z, _, core = place(ctx, head)
    return device(y, core * 4 + (z % 4 + 2) % 4, x0, z // 4)


def me():
    return lax.axis_index("ctx"), lax.axis_index("head")


def signal(barrier, target):
    pl.semaphore_signal(barrier, inc=1, device_id=target, device_id_type=MESH)


def remote(src, dst, send, recv, target):
    return pltpu.make_async_remote_copy(
        src_ref=src, dst_ref=dst, send_sem=send, recv_sem=recv, device_id=target, device_id_type=MESH
    )


class Stream:
    def __init__(self, count, dst, src, slot, own):
        self.count, self.dst, self.src, self.slot, self.own = count, dst, src, slot, own


def home_stream():
    ctx, head = me()
    return Stream(4, lambda i: home_of(ctx, head, i), lambda k: owner_of(ctx, head, k), ctx % 4, None)


def owner_stream():
    ctx, head = me()
    return Stream(4, lambda i: owner_of(ctx, head, i), lambda k: home_of(ctx, head, k), ctx % 4, None)


def group_stream():
    ctx, head = me()
    return Stream(
        8, lambda i: member(ctx, head, i), lambda k: member(ctx, head, k), chunk_of(ctx, head), chunk_of(ctx, head)
    )


def plane_stream():
    ctx, head = me()
    y, z, x, core = place(ctx, head)

    def at(r):
        return device(y, r // 4 % 2 * 4 + r // 8, (r + 3) % 4, core)

    rank = z % 4 * 8 + z // 4 * 4 + (x + 1) % 4
    return Stream(32, at, at, rank, rank)


def rows_stream():
    ctx, head = me()
    _, z, x, _ = place(ctx, head)
    r = z % 4 * 8 + z // 4 * 4 + (x + 1) % 4

    def src(k):
        return device(k // 2, ctx // 4 % 2 * 4 + ctx // 8, (ctx + 3) % 4, k % 2)

    return Stream(8, lambda i: (r, i), src, chunk_of(ctx, head), None)


def dot(a, b, contract):
    return lax.dot_general(a, b, ((contract[0], contract[1]), ((), ())), preferred_element_type=F32)


class Refs:
    def __init__(self, names, refs):
        for name, ref in zip(names, refs, strict=True):
            setattr(self, name, ref)


def greet_all(r, barrier):
    ctx, head = me()
    j = chunk_of(ctx, head)
    homes, owners, rows, plane = home_stream(), owner_stream(), rows_stream(), plane_stream()
    for k in range(4):
        signal(barrier, homes.src(k))
        signal(barrier, owners.src(k))
    for d in range(1, 8):
        signal(barrier, member(ctx, head, (j + d) % 8))
    for k in range(8):
        signal(barrier, rows.src(k))

    def greet(d, carry):
        signal(barrier, plane.src((plane.own + d) % 32))
        return carry

    lax.fori_loop(1, 32, greet, 0)


def front(r):
    ctx, head = me()
    j = chunk_of(ctx, head)
    core = j % 2
    homes = home_stream()
    sibling = j + 1 - 2 * core
    up, down, far = (j + 2) % 8, (j + 6) % 8, (j + 4) % 8

    def block_copy(k, half, slot):
        part = pl.ds(32 * half, 32)
        return remote(
            r.x.at[k, part], r.home.at[slot, part], r.x_send.at[half, k], r.x_recv.at[half, slot], homes.dst(k)
        )

    for k in range(4):
        block_copy(k, 0, homes.slot).start()
    for k in range(4):
        r.c_buf[k] = jnp.zeros((8, 128), F32)
        r.c_buf[k, 0:1, 0:64] = r.curvature[k : k + 1, :]
        remote(r.c_buf.at[k], r.c_home.at[homes.slot], r.c_send.at[k], r.c_recv.at[homes.slot], homes.dst(k)).start()

    def columns(weight, size, at, factor):
        shape = (weight.shape[1], 384)
        row = lax.broadcasted_iota(jnp.int32, shape, 0)
        column = lax.broadcasted_iota(jnp.int32, shape, 1)
        hit = (row - j * size == column - at) & (column >= at) & (column < at + size)
        return dot(weight[...], jnp.where(hit, factor, 0.0).astype(BF16), ((1,), (0,)))

    def join(joined, names):
        for name, size, at, factor in names:
            fetch(r, name).wait()
            part = columns(getattr(r, name), size, at, factor)
            joined = part if joined is None else joined + part
        return joined

    def piece(i, p):
        return r.normed.at[i, pl.ds(p % 4 * 64 + p // 4 * 32, 32)]

    def push(i, p, way, to):
        remote(piece(i, p), piece(i, p), r.n_send.at[i, p, way], r.n_recv.at[i, p], member(ctx, head, to)).start()

    def arrived(i, p):
        remote(
            piece(i, p), piece(i, p), r.n_send.at[i, p, 0], r.n_recv.at[i, p], member(ctx, head, sibling)
        ).wait_recv()

    def sent(i, p, way, to):
        remote(piece(i, p), piece(i, p), r.n_send.at[i, p, way], r.n_recv.at[i, p], member(ctx, head, to)).wait_send()

    gain = r.gain[...].reshape(1, -1)
    def norm(p):
        k, half = p % 4, p // 4
        block_copy(k, half, k).wait_recv()
        inputs = r.home[k, 32 * half : 32 * half + 32, :].astype(F32)
        spread = jnp.sqrt(jnp.mean(inputs * inputs, axis=-1, keepdims=True) + 1e-06)
        at = 64 * k + 32 * half
        r.normed[j, at : at + 32, :] = (inputs / spread * gain).astype(BF16)
        push(j, p, 1, up)
        push(j, p, 2, down)
        push(j, p, 0, sibling)

    joined = join(None, (("tq", KEY, 0, SCALE), ("wq", KEY, KEY, SCALE)))
    for k in range(4):
        block_copy(k, 0, homes.slot).wait_send()
        block_copy(k, 1, homes.slot).start()
    for p in range(4):
        norm(p)
    joined = join(joined, (("wk", KEY, 2 * KEY, 1.0), ("tk", KEY, 3 * KEY, 1.0), ("wv", VAL, 4 * KEY, 1.0)))
    r.joined[...] = joined.astype(BF16)
    for p in range(4, 8):
        norm(p)

    def project(i):
        rows = pl.ds(pl.multiple_of(i * BLOCK, BLOCK), BLOCK)
        proj = dot(r.normed[i], r.joined[...], ((1,), (0,))).astype(BF16)
        r.qt[rows, :] = proj[:, :128]
        r.kt[rows, :] = proj[:, 128:256]
        lane = lax.broadcasted_iota(jnp.int32, (BLOCK, 128), 1)
        r.v[rows, :] = jnp.where(lane < VAL, proj[:, 256:].astype(F32), 1.0).astype(BF16)

    project(j)
    for p in range(8):
        arrived(down, p)
        if p % 2 == 0:
            push(down, p, 1, up)
        push(down, p, 0, sibling)
        arrived(up, p)
        if p % 2 == 1:
            push(up, p, 2, down)
        push(up, p, 0, sibling)
    for p in range(8):
        arrived(far, p)
        push(far, p, 0, sibling)
        if p == 3:
            project(down)
        if p == 5:
            project(up)
    for p in range(8):
        arrived(sibling, p)
    project(sibling)
    project(far)
    for d in (2, 6, 4):
        i = (sibling + d) % 8
        for p in range(8):
            arrived(i, p)
        project(i)
    for k in range(4):
        block_copy(k, 1, k).wait_send()
        remote(r.c_buf.at[k], r.c_home.at[k], r.c_send.at[k], r.c_recv.at[k], homes.dst(k)).wait()
    for p in range(8):
        sent(j, p, 1, up)
        sent(j, p, 2, down)
        for i in (j, up, down, far):
            sent(i, p, 0, sibling)
        if p % 2 == 0:
            sent(down, p, 1, up)
        else:
            sent(up, p, 2, down)


def attend_forward(r):
    ctx, head = me()
    j = chunk_of(ctx, head)

    def block(t, carry):
        i = (j + 1 + t) % 8
        rows = pl.ds(pl.multiple_of(i * BLOCK, BLOCK), BLOCK)
        qt = r.qt[rows, :]
        s = dot(qt[:, KEY:], r.kt[:, :KEY], ((1,), (1,)))
        top = jnp.max(s, axis=1, keepdims=True)
        p = jnp.exp(s - top)
        ext = dot(p.astype(BF16), r.v[...], ((1,), (0,)))
        total = ext[:, VAL : VAL + 1]
        inv = 1.0 / total
        ts = dot(qt, r.kt[...], ((1,), (1,)))
        mean = jnp.sum(p * ts, axis=1, keepdims=True) / jnp.sum(p, axis=1, keepdims=True)
        tw = p * (ts - mean)
        tan = dot(tw.astype(BF16), r.v[...], ((1,), (0,))) * inv
        att = ext * inv

        @pl.when(t < 7)
        def _():
            r.att_buf[i, 0] = att[:, :VAL].astype(BF16)
            r.att_buf[i, 1] = tan[:, :VAL].astype(BF16)
            remote(
                r.att_buf.at[i], r.attended.at[j], r.a_send.at[i], r.a_recv.at[j], member(ctx, head, i)
            ).start()

        @pl.when(t == 7)
        def _():
            r.attended[j, 0] = att[:, :VAL].astype(BF16)
            r.attended[j, 1] = tan[:, :VAL].astype(BF16)

        r.att[rows, :] = att
        r.lse[:, rows] = jnp.broadcast_to(top + jnp.log(total), (BLOCK, 128)).T[:8]
        return carry

    lax.fori_loop(0, 8, block, 0)

    def end(t, carry):
        i = (j + 1 + t) % 8
        remote(r.att_buf.at[i], r.attended.at[i], r.a_send.at[i], r.a_recv.at[i], member(ctx, head, i)).wait()
        return carry

    lax.fori_loop(0, 7, end, 0)


def gelu_pair(v):
    root = 0.7978845608028654
    square = v * v
    t = jnp.tanh(root * (v + 0.044715 * v * square))
    half = 0.5 * (1.0 + t)
    return v * half, half + 0.5 * v * (1.0 - t * t) * (root + (3.0 * 0.044715 * root) * square)


def one_hot(shape, wanted):
    column = lax.broadcasted_iota(jnp.int32, shape, 1)
    return jnp.where(column == wanted, 1.0, 0.0).astype(BF16)


def pickers(dilation, rows):
    shape = (2 * rows, rows)
    row = lax.broadcasted_iota(jnp.int32, shape, 0)
    own = one_hot(shape, jnp.where(row < rows, row - dilation, row - rows + dilation))
    edge = lax.broadcasted_iota(jnp.int32, (DMAX, DMAX), 0)
    return own, one_hot((DMAX, DMAX), edge + DMAX - dilation), one_hot((DMAX, DMAX), edge + dilation - DMAX)


def conv_chain(r):
    ctx, head = me()
    j = chunk_of(ctx, head)
    rows, features, width = BLOCK, r.w_out.shape[1], r.conv.shape[3]
    owners = owner_stream()

    def beside(step):
        return member(ctx, head, (j + step + 8) % 8)

    def swap(n, cells, halo):
        lead = (slice(None),) * (len(cells.shape) - 2)
        first = cells.at[lead + (pl.ds(0, DMAX), slice(None))]
        last = cells.at[lead + (pl.ds(rows - DMAX, DMAX), slice(None))]
        down = remote(first, halo.at[1], r.h_send.at[2 * n], r.h_recv.at[2 * n], beside(-1))
        up = remote(last, halo.at[0], r.h_send.at[2 * n + 1], r.h_recv.at[2 * n + 1], beside(1))

        @pl.when(j > 0)
        def _():
            down.start()

        @pl.when(j < 7)
        def _():
            up.start()

        def finish():
            @pl.when(j > 0)
            def _():
                up.wait_recv()
                down.wait_send()

            @pl.when(j == 0)
            def _():
                halo[0] = jnp.zeros(halo.shape[1:], BF16)

            @pl.when(j < 7)
            def _():
                down.wait_recv()
                up.wait_send()

            @pl.when(j == 7)
            def _():
                halo[1] = jnp.zeros(halo.shape[1:], BF16)

        return finish

    for name in ("w_out", "conv", "point"):
        fetch(r, name).wait()
    both = jnp.zeros((2 * rows, features), F32)
    for h in range(HEADS):
        both = both + dot(r.attended[h].reshape(2 * rows, VAL), r.w_out[h * VAL : (h + 1) * VAL, :], ((1,), (0,)))
    r.mixed[...] = r.home[...].reshape(rows, features).astype(F32) + both[:rows]
    r.tan[...] = both[rows:]
    for layer in range(2):
        dilation = r.dilations[layer]
        act, slope = gelu_pair(r.mixed[...])
        r.slope[layer] = slope
        cells, halo, conv = r.act.at[layer], r.halo.at[layer], r.conv.at[layer]
        cells[0] = act.astype(BF16)
        cells[1] = (slope * r.tan[...]).astype(BF16)
        finish = swap(layer, cells, halo)
        inner = dot(cells[...].reshape(2 * rows, features), conv[1], ((1,), (0,)))
        pick, pick_low, pick_high = pickers(dilation, rows)
        value = dot(pick, cells[0], ((1,), (0,))).astype(BF16)
        tangent = dot(pick, cells[1], ((1,), (0,))).astype(BF16)
        for n, tap in ((0, 0), (1, 2)):
            window = jnp.concatenate([value[n * rows : (n + 1) * rows], tangent[n * rows : (n + 1) * rows]], axis=0)
            inner = inner + dot(window, conv[tap], ((1,), (0,)))
        r.inner[...] = inner.reshape(2, rows, width)
        finish()
        for n, tap, pick, at in ((0, 0, pick_low, 0), (1, 2, pick_high, rows - DMAX)):
            window = jnp.concatenate([dot(pick, halo[n, m], ((1,), (0,))).astype(BF16) for m in range(2)], axis=0)
            r.inner[:, at : at + DMAX, :] += dot(window, conv[tap], ((1,), (0,))).reshape(2, DMAX, width)
        hidden, hslope = gelu_pair(r.inner[0])
        r.hslope[layer] = hslope
        hidden = jnp.concatenate([hidden, hslope * r.inner[1]], axis=0).astype(BF16)
        point = dot(hidden, r.point[layer], ((1,), (0,)))
        if layer == 0:
            r.mixed[...] += point[:rows]
        r.tan[...] += point[rows:]
    r.out_buf[0] = r.tan[...].astype(BF16)
    for k in range(4):
        out_copy(r, 0, k, owners.slot, owners.dst(k)).start()
    for k in range(4):
        curve = r.c_home[k].T[:64, 0:1]
        at = slice(64 * k, 64 * k + 64)
        r.grad[at, :] = curve * r.tan[at, :]
    for layer in (1, 0):
        dilation = r.dilations[layer]
        back = dot(r.grad[...].astype(BF16), r.point[layer], ((1,), (1,)))
        cells, halo, conv = r.gact.at[layer], r.ghalo.at[layer], r.conv.at[layer]
        cells[...] = (back * r.hslope[layer]).astype(BF16)
        finish = swap(2 + layer, cells, halo)
        act = dot(cells[...], conv[1], ((1,), (1,)))
        pick, pick_low, pick_high = pickers(dilation, rows)
        windows = dot(pick, cells[...], ((1,), (0,))).astype(BF16)
        act = act + dot(windows[:rows], conv[2], ((1,), (1,)))
        act = act + dot(windows[rows:], conv[0], ((1,), (1,)))
        r.grad[...] += r.slope[layer] * act
        finish()
        for n, tap, pick, at in ((0, 2, pick_low, 0), (1, 0, pick_high, rows - DMAX)):
            window = dot(pick, halo[n], ((1,), (0,))).astype(BF16)
            at = slice(at, at + DMAX)
            r.grad[at, :] += r.slope[layer, at, :] * dot(window, conv[tap], ((1,), (1,)))
    final = r.grad[...].astype(BF16)

    def send(t, carry):
        i = (j + 1 + t) % 8
        part = r.w_out[pl.ds(pl.multiple_of(i * VAL, 32), VAL), :]
        ga = dot(final, part, ((1,), (1,))).astype(BF16)

        @pl.when(t < 7)
        def _():
            r.ga_buf[i] = ga
            remote(r.ga_buf.at[i], r.item.at[j], r.g_send.at[i], r.g_recv.at[j], member(ctx, head, i)).start()

        @pl.when(t == 7)
        def _():
            r.item[j] = ga

        return carry

    lax.fori_loop(0, 8, send, 0)


def out_copy(r, n, k, slot, target):
    out = (r.out_t, r.out_c)[n]
    return remote(
        r.out_buf.at[n, pl.ds(64 * k, 64)], out.at[slot], r.o_send.at[n, k], r.o_recv.at[n, slot], target
    )


def back(r):
    ctx, head = me()
    j = chunk_of(ctx, head)
    owners, rows, plane = owner_stream(), rows_stream(), plane_stream()
    length = 8 * BLOCK
    r.q[...] = r.qt[:, KEY:]
    r.acc[...] = jnp.zeros(r.acc.shape, F32)
    for c in range(8):
        at = slice(c * BLOCK, (c + 1) * BLOCK)
        r.kT[:, at] = (r.kt[at, :].astype(F32).T[:KEY] * SCALE).astype(BF16)

    def ga_end(t, carry):
        i = (j + 1 + t) % 8
        remote(r.ga_buf.at[i], r.item.at[i], r.g_send.at[i], r.g_recv.at[i], member(ctx, head, i)).wait()
        return carry

    lax.fori_loop(0, 7, ga_end, 0)
    for c in range(8):
        at = slice(c * BLOCK, (c + 1) * BLOCK)
        prod = r.item[c].astype(F32) * r.att[at, :VAL]
        prod = jnp.concatenate([prod, jnp.zeros((BLOCK, 128 - VAL), F32)], axis=1)
        r.delta[:, at] = jnp.broadcast_to(jnp.sum(prod.T, axis=0, keepdims=True), (8, BLOCK))

    def packed(a):
        return jnp.concatenate([a[: BLOCK // 2], a[BLOCK // 2 :]], axis=1)

    def deliver(buf, ref, send, recv, i, t, value):
        @pl.when(t < 7)
        def _():
            buf[i] = value
            remote(buf.at[i], ref.at[j], send.at[i], recv.at[j], member(ctx, head, i)).start()

        @pl.when(t == 7)
        def _():
            ref[j] = value

    def block(t, carry):
        i = (j + 1 + t) % 8
        at = pl.ds(pl.multiple_of(i * BLOCK, BLOCK), BLOCK)
        g = r.item[...].reshape(length, VAL)
        s = dot(r.kt[at, :KEY], r.q[...], ((1,), (1,)))
        w = jnp.exp(s - r.lse[0:1, :])
        dp = dot(r.v[at, :VAL], g, ((1,), (1,)))
        ds = (w * (dp - r.delta[0:1, :])).astype(BF16)
        dv = dot(w.astype(BF16), g, ((1,), (0,))).astype(BF16)
        deliver(r.dv_buf, r.dv, r.v_send, r.v_recv, i, t, dv)
        dk = packed(dot(ds, r.q[...], ((1,), (0,))))
        deliver(r.dk_buf, r.dk, r.k_send, r.k_recv, i, t, dk.astype(BF16))
        dkT = dk.T
        r.pairT[KEY:, at] = jnp.concatenate([dkT[:KEY], dkT[KEY:]], axis=1).astype(BF16)
        r.acc[...] += dot(r.kT[:, at], ds, ((1,), (0,)))
        return carry

    lax.fori_loop(0, 8, block, 0)

    def dq_out(t, carry):
        i = (j + 1 + t) % 8
        at = pl.ds(pl.multiple_of(i * BLOCK, BLOCK), BLOCK)
        part = r.acc[:, at]
        dq = jnp.concatenate([part[:, : BLOCK // 2], part[:, BLOCK // 2 :]], axis=0).T.astype(BF16)
        deliver(r.dq_buf, r.dq, r.q_send, r.q_recv, i, t, dq)
        return carry

    lax.fori_loop(0, 8, dq_out, 0)
    r.pairT[:KEY, :] = r.acc[...].astype(BF16)
    part = dot(r.pairT[...], r.normed[...].reshape(length, -1), ((1,), (0,)))
    r.part_buf[...] = part.T.reshape(r.part_buf.shape)
    r.part[plane.own] = r.part_buf[plane.own]

    def part_out(d, carry):
        k = (plane.own + d) % 32
        remote(r.part_buf.at[k], r.part.at[plane.slot], r.e_send.at[k], r.e_recv.at[plane.slot], plane.dst(k)).start()
        return carry

    lax.fori_loop(1, 32, part_out, 0)

    def early_end(t, carry):
        i = (j + 1 + t) % 8
        to = member(ctx, head, i)
        remote(r.dv_buf.at[i], r.dv.at[i], r.v_send.at[i], r.v_recv.at[i], to).wait()
        remote(r.dk_buf.at[i], r.dk.at[i], r.k_send.at[i], r.k_recv.at[i], to).wait()
        return carry

    lax.fori_loop(0, 7, early_end, 0)
    inputs = r.home[...].reshape(BLOCK, -1).astype(F32)
    count, features = inputs.shape

    def unpacked(a, b):
        top = jnp.concatenate([a[:, :KEY], b[:, :KEY]], axis=1)
        return jnp.concatenate([top, jnp.concatenate([a[:, KEY:], b[:, KEY:]], axis=1)], axis=0)

    acc = jnp.zeros((count, features), F32)
    for h in range(HEADS):
        acc = acc + dot(r.dv[h], r.wv[:, h * VAL : (h + 1) * VAL], ((1,), (1,)))
    for h in range(0, HEADS, 2):
        acc = acc + dot(unpacked(r.dk[h], r.dk[h + 1]), r.wk[:, h * KEY : (h + 2) * KEY], ((1,), (1,)))

    def late_end(t, carry):
        i = (j + 1 + t) % 8
        remote(r.dq_buf.at[i], r.dq.at[i], r.q_send.at[i], r.q_recv.at[i], member(ctx, head, i)).wait()
        return carry

    lax.fori_loop(0, 7, late_end, 0)
    for h in range(0, HEADS, 2):
        acc = acc + dot(unpacked(r.dq[h], r.dq[h + 1]), r.wq[:, h * KEY : (h + 2) * KEY], ((1,), (1,)))
    gained = acc * r.gain[...].reshape(1, -1)
    spread = jnp.sqrt(jnp.mean(inputs * inputs, axis=-1, keepdims=True) + 1e-06)
    along = jnp.sum(gained * inputs, axis=-1, keepdims=True)
    inv = 1.0 / spread
    r.out_buf[1] = (
        r.grad[...] + gained * inv - inputs * (along / (features * spread * spread * spread))
    ).astype(BF16)
    for k in range(4):
        out_copy(r, 1, k, owners.slot, owners.dst(k)).start()

    def part_end(d, carry):
        k = (plane.own + d) % 32
        remote(r.part_buf.at[k], r.part.at[k], r.e_send.at[k], r.e_recv.at[k], plane.dst(k)).wait()
        return carry

    lax.fori_loop(1, 32, part_end, 0)
    summed = jnp.sum(r.part[...], axis=0) * (1.0 / (32.0 * 2048.0))
    for k in range(8):
        r.rows[k, 0:3, :] = summed[3 * k : 3 * k + 3, :]
        r.rows[k, 3:8, :] = jnp.zeros((5, 2 * KEY), F32)
    for k in range(8):
        remote(r.rows.at[k], r.got.at[rows.slot], r.r_send.at[k], r.r_recv.at[rows.slot], rows.dst(k)).start()
    for k in range(8):
        remote(r.rows.at[k], r.got.at[k], r.r_send.at[k], r.r_recv.at[k], rows.dst(k)).wait()
    for k in range(8):
        r.gvq[:, k * KEY : (k + 1) * KEY] = r.got[k, 0:3, :KEY]
        r.gvk[:, k * KEY : (k + 1) * KEY] = r.got[k, 0:3, KEY:]
    for n in range(2):
        for k in range(4):
            out_copy(r, n, k, k, owners.dst(k)).wait()


WEIGHTS = ("tq", "wq", "wk", "tk", "wv", "w_out", "conv", "point")


def fetch(r, name):
    n = WEIGHTS.index(name)
    return pltpu.make_async_copy(getattr(r, name + "_hbm"), getattr(r, name), r.w_sem.at[n])


def whole_kernel(names, *refs):
    r = Refs(names, refs)
    barrier = pltpu.get_barrier_semaphore()
    greet_all(r, barrier)
    for name in WEIGHTS:
        fetch(r, name).start()
    pl.semaphore_wait(barrier, 54)
    front(r)
    attend_forward(r)
    conv_chain(r)
    back(r)


def run(inputs, collective_id):
    by_name = {name: array for name, array, _ in inputs}
    features = by_name["x"].shape[2]
    width = by_name["conv_hbm"].shape[3]
    length = 8 * BLOCK
    rows = BLOCK
    vmem, dma = pltpu.VMEM, pltpu.SemaphoreType.DMA
    scratch = {name: vmem(by_name[name + "_hbm"].shape, BF16) for name in WEIGHTS}
    scratch.update(
        w_sem=dma((len(WEIGHTS),)),
        home=vmem((4, 64, features), BF16),
        c_buf=vmem((4, 8, 128), F32),
        c_home=vmem((4, 8, 128), F32),
        joined=vmem((features, 384), BF16),
        normed=vmem((8, rows, features), BF16),
        qt=vmem((length, 128), BF16),
        kt=vmem((length, 128), BF16),
        v=vmem((length, 128), BF16),
        att_buf=vmem((8, 2, rows, VAL), BF16),
        attended=vmem((8, 2, rows, VAL), BF16),
        att=vmem((length, 128), F32),
        lse=vmem((8, length), F32),
        mixed=vmem((rows, features), F32),
        tan=vmem((rows, features), F32),
        grad=vmem((rows, features), F32),
        slope=vmem((2, rows, features), F32),
        hslope=vmem((2, rows, width), F32),
        act=vmem((2, 2, rows, features), BF16),
        inner=vmem((2, rows, width), F32),
        halo=vmem((2, 2, 2, DMAX, features), BF16),
        gact=vmem((2, rows, width), BF16),
        ghalo=vmem((2, 2, DMAX, width), BF16),
        out_buf=vmem((2, rows, features), BF16),
        ga_buf=vmem((8, rows, VAL), BF16),
        item=vmem((8, rows, VAL), BF16),
        q=vmem((length, KEY), BF16),
        kT=vmem((KEY, length), BF16),
        delta=vmem((8, length), F32),
        acc=vmem((KEY, length), F32),
        pairT=vmem((2 * KEY, length), BF16),
        dv_buf=vmem((8, rows, VAL), BF16),
        dv=vmem((8, rows, VAL), BF16),
        dk_buf=vmem((8, rows // 2, 2 * KEY), BF16),
        dk=vmem((8, rows // 2, 2 * KEY), BF16),
        dq_buf=vmem((8, rows // 2, 2 * KEY), BF16),
        dq=vmem((8, rows // 2, 2 * KEY), BF16),
        part_buf=vmem((32, features // 32, 2 * KEY), F32),
        part=vmem((32, features // 32, 2 * KEY), F32),
        rows=vmem((8, 8, 2 * KEY), F32),
        got=vmem((8, 8, 2 * KEY), F32),
    )
    for name, shape in (
        ("x", (2, 4)),
        ("c", (4,)),
        ("n", (8, 8)),
        ("a", (8,)),
        ("h", (8,)),
        ("o", (2, 4)),
        ("g", (8,)),
        ("v", (8,)),
        ("k", (8,)),
        ("q", (8,)),
        ("e", (32,)),
        ("r", (8,)),
    ):
        scratch[name + "_send"] = dma(shape + (3,)) if name == "n" else dma(shape)
        scratch[name + "_recv"] = dma(shape)
    outs = ("out_t", "out_c", "gvq", "gvk")
    names = [name for name, _, _ in inputs] + list(outs) + list(scratch)
    return pl.pallas_call(
        functools.partial(whole_kernel, names),
        out_shape=[
            jax.ShapeDtypeStruct((4, 64, features), BF16),
            jax.ShapeDtypeStruct((4, 64, features), BF16),
            jax.ShapeDtypeStruct((3, HEADS * KEY), F32),
            jax.ShapeDtypeStruct((3, HEADS * KEY), F32),
        ],
        in_specs=[pl.BlockSpec(memory_space=space) for _, _, space in inputs],
        out_specs=[pl.BlockSpec(memory_space=space) for space in (pl.ANY, pl.ANY, vmem, vmem)],
        scratch_shapes=list(scratch.values()),
        compiler_params=pltpu.CompilerParams(
            collective_id=collective_id, has_side_effects=True, vmem_limit_bytes=VMEM_LIMIT
        ),
    )(*[array for _, array, _ in inputs])


def deliver_kernel(*refs):
    count = len(refs) // 2
    for n in range(count):
        refs[count + n][...] = refs[n][...]


def deliver_all(arrays):
    return pl.pallas_call(
        deliver_kernel,
        out_shape=[jax.ShapeDtypeStruct(a.shape, a.dtype) for a in arrays],
        in_specs=[pl.BlockSpec(memory_space=pltpu.VMEM)] * len(arrays),
        out_specs=[pl.BlockSpec(memory_space=pltpu.VMEM)] * len(arrays),
    )(*arrays)


def per_device(
    window_input,
    norm_gain,
    w_query,
    w_key,
    w_value,
    w_out,
    conv_weight,
    point_weight,
    dilations,
    tangent_query,
    tangent_key,
    curvature,
):
    outs = run(
        (
            ("dilations", dilations, pltpu.SMEM),
            ("x", window_input, pl.ANY),
            ("curvature", curvature, pltpu.VMEM),
            ("gain", norm_gain, pltpu.VMEM),
            ("tq_hbm", tangent_query, pl.ANY),
            ("wq_hbm", w_query, pl.ANY),
            ("wk_hbm", w_key, pl.ANY),
            ("tk_hbm", tangent_key, pl.ANY),
            ("wv_hbm", w_value, pl.ANY),
            ("w_out_hbm", w_out, pl.ANY),
            ("conv_hbm", conv_weight, pl.ANY),
            ("point_hbm", point_weight, pl.ANY),
        ),
        0,
    )
    return tuple(deliver_all(outs))


def solution(mesh):
    in_specs = (P("head", "ctx", None),) + (P(),) * 10 + (P("head", "ctx"),)
    out_specs = (
        P("head", "ctx", None),
        P("head", "ctx", None),
        P(("ctx", "head"), None),
        P(("ctx", "head"), None),
    )
    return jax.shard_map(per_device, mesh=mesh, in_specs=in_specs, out_specs=out_specs, check_vma=False)
```

```python
import functools

import jax
import jax.numpy as jnp
from jax import lax
from jax.experimental import pallas as pl
from jax.experimental.pallas import tpu as pltpu
from jax.sharding import PartitionSpec as P

HEADS = 8
KEY = 64
VAL = 96
DMAX = 16
MESH = pl.DeviceIdType.MESH
VMEM_LIMIT = 56 * 2**20
F32 = jnp.float32
BF16 = jnp.bfloat16
BLOCK = 256
SCALE = KEY**-0.5


def place(ctx, head):
    return ctx // 8, (ctx // 4) % 2 * 4 + head // 2, ctx % 4, head % 2


def device(y, z, x, core):
    return y * 8 + z // 4 * 4 + x, z % 4 * 2 + core


def chunk_of(ctx, head):
    return ctx // 8 * 2 + head % 2


def member(ctx, head, j):
    _, z, x, _ = place(ctx, head)
    return device(j // 2, z, x, j % 2)


def home_of(ctx, head, b):
    y, z, _, core = place(ctx, head)
    return device(y, core * 4 + (z % 4 + 2) % 4, b, z // 4)


def owner_of(ctx, head, x0):
    y, z, _, core = place(ctx, head)
    return device(y, core * 4 + (z % 4 + 2) % 4, x0, z // 4)


def me():
    return lax.axis_index("ctx"), lax.axis_index("head")


def signal(barrier, target):
    pl.semaphore_signal(barrier, inc=1, device_id=target, device_id_type=MESH)


def remote(src, dst, send, recv, target):
    return pltpu.make_async_remote_copy(
        src_ref=src, dst_ref=dst, send_sem=send, recv_sem=recv, device_id=target, device_id_type=MESH
    )


class Stream:
    def __init__(self, count, dst, src, slot, own):
        self.count, self.dst, self.src, self.slot, self.own = count, dst, src, slot, own


def home_stream():
    ctx, head = me()
    return Stream(4, lambda i: home_of(ctx, head, i), lambda k: owner_of(ctx, head, k), ctx % 4, None)


def owner_stream():
    ctx, head = me()
    return Stream(4, lambda i: owner_of(ctx, head, i), lambda k: home_of(ctx, head, k), ctx % 4, None)


def group_stream():
    ctx, head = me()
    return Stream(
        8, lambda i: member(ctx, head, i), lambda k: member(ctx, head, k), chunk_of(ctx, head), chunk_of(ctx, head)
    )


def line_stream():
    ctx, head = me()
    y, z, x, core = place(ctx, head)

    def at(i):
        return device(y, z, (i + 3) % 4, core)

    return Stream(4, at, at, (x + 1) % 4, (x + 1) % 4)


def column_stream():
    ctx, head = me()
    y, z, x, core = place(ctx, head)

    def at(m):
        return device(y, m % 2 * 4 + m // 2, x, core)

    rank = z % 4 * 2 + z // 4
    return Stream(8, at, at, rank, rank)


def rows_stream():
    ctx, head = me()
    _, z, x, _ = place(ctx, head)
    r = z % 4 * 8 + z // 4 * 4 + (x + 1) % 4

    def src(k):
        return device(k // 2, ctx // 4 % 2 * 4 + ctx // 8, (ctx + 3) % 4, k % 2)

    return Stream(8, lambda i: (r, i), src, chunk_of(ctx, head), None)


def dot(a, b, contract):
    return lax.dot_general(a, b, ((contract[0], contract[1]), ((), ())), preferred_element_type=F32)


class Refs:
    def __init__(self, names, refs):
        for name, ref in zip(names, refs, strict=True):
            setattr(self, name, ref)


def greet_all(r, barrier):
    ctx, head = me()
    j = chunk_of(ctx, head)
    homes, owners, rows = home_stream(), owner_stream(), rows_stream()
    line, column = line_stream(), column_stream()
    for k in range(4):
        signal(barrier, homes.src(k))
        signal(barrier, owners.src(k))
    for d in range(1, 8):
        signal(barrier, member(ctx, head, (j + d) % 8))
        signal(barrier, column.src((column.own + d) % 8))
    for d in range(1, 4):
        signal(barrier, line.src((line.own + d) % 4))
    for k in range(8):
        signal(barrier, rows.src(k))


def front(r):
    ctx, head = me()
    j = chunk_of(ctx, head)
    core = j % 2
    homes = home_stream()
    sibling = j + 1 - 2 * core
    up, down, far = (j + 2) % 8, (j + 6) % 8, (j + 4) % 8

    def block_copy(k, half, slot):
        part = pl.ds(32 * half, 32)
        return remote(
            r.x.at[k, part], r.home.at[slot, part], r.x_send.at[half, k], r.x_recv.at[half, slot], homes.dst(k)
        )

    for k in range(4):
        block_copy(k, 0, homes.slot).start()
    for k in range(4):
        r.c_buf[k] = jnp.zeros((8, 128), F32)
        r.c_buf[k, 0:1, 0:64] = r.curvature[k : k + 1, :]
        remote(r.c_buf.at[k], r.c_home.at[homes.slot], r.c_send.at[k], r.c_recv.at[homes.slot], homes.dst(k)).start()

    def columns(weight, size, at, factor):
        shape = (weight.shape[1], 384)
        row = lax.broadcasted_iota(jnp.int32, shape, 0)
        column = lax.broadcasted_iota(jnp.int32, shape, 1)
        hit = (row - j * size == column - at) & (column >= at) & (column < at + size)
        return dot(weight[...], jnp.where(hit, factor, 0.0).astype(BF16), ((1,), (0,)))

    def join(joined, names):
        for name, size, at, factor in names:
            fetch(r, name).wait()
            part = columns(getattr(r, name), size, at, factor)
            joined = part if joined is None else joined + part
        return joined

    def piece(i, p):
        return r.normed.at[i, pl.ds(p % 4 * 64 + p // 4 * 32, 32)]

    def push(i, p, way, to):
        remote(piece(i, p), piece(i, p), r.n_send.at[i, p, way], r.n_recv.at[i, p], member(ctx, head, to)).start()

    def arrived(i, p):
        remote(
            piece(i, p), piece(i, p), r.n_send.at[i, p, 0], r.n_recv.at[i, p], member(ctx, head, sibling)
        ).wait_recv()

    def sent(i, p, way, to):
        remote(piece(i, p), piece(i, p), r.n_send.at[i, p, way], r.n_recv.at[i, p], member(ctx, head, to)).wait_send()

    gain = r.gain[...].reshape(1, -1)
    def norm(p):
        k, half = p % 4, p // 4
        block_copy(k, half, k).wait_recv()
        inputs = r.home[k, 32 * half : 32 * half + 32, :].astype(F32)
        spread = jnp.sqrt(jnp.mean(inputs * inputs, axis=-1, keepdims=True) + 1e-06)
        at = 64 * k + 32 * half
        r.normed[j, at : at + 32, :] = (inputs / spread * gain).astype(BF16)
        push(j, p, 1, up)
        push(j, p, 2, down)
        push(j, p, 0, sibling)

    joined = join(None, (("tq", KEY, 0, SCALE), ("wq", KEY, KEY, SCALE)))
    for k in range(4):
        block_copy(k, 0, homes.slot).wait_send()
        block_copy(k, 1, homes.slot).start()
    for p in range(4):
        norm(p)
    joined = join(joined, (("wk", KEY, 2 * KEY, 1.0), ("tk", KEY, 3 * KEY, 1.0), ("wv", VAL, 4 * KEY, 1.0)))
    r.joined[...] = joined.astype(BF16)
    for name in WEIGHTS[5:]:
        fetch(r, name).start()
    for p in range(4, 8):
        norm(p)

    def project(i):
        rows = pl.ds(pl.multiple_of(i * BLOCK, BLOCK), BLOCK)
        proj = dot(r.normed[i], r.joined[...], ((1,), (0,))).astype(BF16)
        r.qt[rows, :] = proj[:, :128]
        r.kt[rows, :] = proj[:, 128:256]
        lane = lax.broadcasted_iota(jnp.int32, (BLOCK, 128), 1)
        r.v[rows, :] = jnp.where(lane < VAL, proj[:, 256:].astype(F32), 1.0).astype(BF16)

    project(j)
    for p in range(8):
        arrived(down, p)
        if p % 2 == 0:
            push(down, p, 1, up)
        push(down, p, 0, sibling)
        arrived(up, p)
        if p % 2 == 1:
            push(up, p, 2, down)
        push(up, p, 0, sibling)
    for p in range(8):
        arrived(far, p)
        push(far, p, 0, sibling)
        if p == 3:
            project(down)
        if p == 5:
            project(up)
    for p in range(8):
        arrived(sibling, p)
    project(sibling)
    project(far)
    for d in (2, 6, 4):
        i = (sibling + d) % 8
        for p in range(8):
            arrived(i, p)
        project(i)
    for k in range(4):
        block_copy(k, 1, k).wait_send()
        remote(r.c_buf.at[k], r.c_home.at[k], r.c_send.at[k], r.c_recv.at[k], homes.dst(k)).wait()
    for p in range(8):
        sent(j, p, 1, up)
        sent(j, p, 2, down)
        for i in (j, up, down, far):
            sent(i, p, 0, sibling)
        if p % 2 == 0:
            sent(down, p, 1, up)
        else:
            sent(up, p, 2, down)


def attend_forward(r):
    ctx, head = me()
    j = chunk_of(ctx, head)

    def block(t, carry):
        i = (j + 1 + t) % 8
        rows = pl.ds(pl.multiple_of(i * BLOCK, BLOCK), BLOCK)
        qt = r.qt[rows, :]
        s = dot(qt[:, KEY:], r.kt[:, :KEY], ((1,), (1,)))
        top = jnp.max(s, axis=1, keepdims=True)
        p = jnp.exp(s - top)
        ext = dot(p.astype(BF16), r.v[...], ((1,), (0,)))
        total = ext[:, VAL : VAL + 1]
        inv = 1.0 / total
        ts = dot(qt, r.kt[...], ((1,), (1,)))
        mean = jnp.sum(p * ts, axis=1, keepdims=True) / jnp.sum(p, axis=1, keepdims=True)
        tw = p * (ts - mean)
        tan = dot(tw.astype(BF16), r.v[...], ((1,), (0,))) * inv
        att = ext * inv

        @pl.when(t < 7)
        def _():
            r.att_buf[i, 0] = att[:, :VAL].astype(BF16)
            r.att_buf[i, 1] = tan[:, :VAL].astype(BF16)
            remote(
                r.att_buf.at[i], r.attended.at[j], r.a_send.at[i], r.a_recv.at[j], member(ctx, head, i)
            ).start()

        @pl.when(t == 7)
        def _():
            r.attended[j, 0] = att[:, :VAL].astype(BF16)
            r.attended[j, 1] = tan[:, :VAL].astype(BF16)

        r.att[rows, :] = att
        r.lse[:, rows] = jnp.broadcast_to(top + jnp.log(total), (BLOCK, 128)).T[:8]
        return carry

    lax.fori_loop(0, 8, block, 0)

    def end(t, carry):
        i = (j + 1 + t) % 8
        remote(r.att_buf.at[i], r.attended.at[i], r.a_send.at[i], r.a_recv.at[i], member(ctx, head, i)).wait()
        return carry

    lax.fori_loop(0, 7, end, 0)


def gelu_pair(v):
    root = 0.7978845608028654
    square = v * v
    t = jnp.tanh(root * (v + 0.044715 * v * square))
    half = 0.5 * (1.0 + t)
    return v * half, half + 0.5 * v * (1.0 - t * t) * (root + (3.0 * 0.044715 * root) * square)


def one_hot(shape, wanted):
    column = lax.broadcasted_iota(jnp.int32, shape, 1)
    return jnp.where(column == wanted, 1.0, 0.0).astype(BF16)


def pickers(dilation, rows):
    shape = (2 * rows, rows)
    row = lax.broadcasted_iota(jnp.int32, shape, 0)
    own = one_hot(shape, jnp.where(row < rows, row - dilation, row - rows + dilation))
    edge = lax.broadcasted_iota(jnp.int32, (DMAX, DMAX), 0)
    return own, one_hot((DMAX, DMAX), edge + DMAX - dilation), one_hot((DMAX, DMAX), edge + dilation - DMAX)


def conv_chain(r):
    ctx, head = me()
    j = chunk_of(ctx, head)
    rows, features, width = BLOCK, r.w_out.shape[1], r.conv.shape[3]
    owners = owner_stream()

    def beside(step):
        return member(ctx, head, (j + step + 8) % 8)

    def swap(n, cells, halo):
        lead = (slice(None),) * (len(cells.shape) - 2)
        first = cells.at[lead + (pl.ds(0, DMAX), slice(None))]
        last = cells.at[lead + (pl.ds(rows - DMAX, DMAX), slice(None))]
        down = remote(first, halo.at[1], r.h_send.at[2 * n], r.h_recv.at[2 * n], beside(-1))
        up = remote(last, halo.at[0], r.h_send.at[2 * n + 1], r.h_recv.at[2 * n + 1], beside(1))

        @pl.when(j > 0)
        def _():
            down.start()

        @pl.when(j < 7)
        def _():
            up.start()

        def finish():
            @pl.when(j > 0)
            def _():
                up.wait_recv()
                down.wait_send()

            @pl.when(j == 0)
            def _():
                halo[0] = jnp.zeros(halo.shape[1:], BF16)

            @pl.when(j < 7)
            def _():
                down.wait_recv()
                up.wait_send()

            @pl.when(j == 7)
            def _():
                halo[1] = jnp.zeros(halo.shape[1:], BF16)

        return finish

    for name in ("w_out", "conv", "point"):
        fetch(r, name).wait()
    both = jnp.zeros((2 * rows, features), F32)
    for h in range(HEADS):
        both = both + dot(r.attended[h].reshape(2 * rows, VAL), r.w_out[h * VAL : (h + 1) * VAL, :], ((1,), (0,)))
    r.mixed[...] = r.home[...].reshape(rows, features).astype(F32) + both[:rows]
    r.tan[...] = both[rows:]
    for layer in range(2):
        dilation = r.dilations[layer]
        act, slope = gelu_pair(r.mixed[...])
        r.slope[layer] = slope
        cells, halo, conv = r.act.at[layer], r.halo.at[layer], r.conv.at[layer]
        cells[0] = act.astype(BF16)
        cells[1] = (slope * r.tan[...]).astype(BF16)
        finish = swap(layer, cells, halo)
        inner = dot(cells[...].reshape(2 * rows, features), conv[1], ((1,), (0,)))
        pick, pick_low, pick_high = pickers(dilation, rows)
        value = dot(pick, cells[0], ((1,), (0,))).astype(BF16)
        tangent = dot(pick, cells[1], ((1,), (0,))).astype(BF16)
        for n, tap in ((0, 0), (1, 2)):
            window = jnp.concatenate([value[n * rows : (n + 1) * rows], tangent[n * rows : (n + 1) * rows]], axis=0)
            inner = inner + dot(window, conv[tap], ((1,), (0,)))
        r.inner[...] = inner.reshape(2, rows, width)
        finish()
        for n, tap, pick, at in ((0, 0, pick_low, 0), (1, 2, pick_high, rows - DMAX)):
            window = jnp.concatenate([dot(pick, halo[n, m], ((1,), (0,))).astype(BF16) for m in range(2)], axis=0)
            r.inner[:, at : at + DMAX, :] += dot(window, conv[tap], ((1,), (0,))).reshape(2, DMAX, width)
        hidden, hslope = gelu_pair(r.inner[0])
        r.hslope[layer] = hslope
        hidden = jnp.concatenate([hidden, hslope * r.inner[1]], axis=0).astype(BF16)
        point = dot(hidden, r.point[layer], ((1,), (0,)))
        if layer == 0:
            r.mixed[...] += point[:rows]
        r.tan[...] += point[rows:]
    r.out_buf[0] = r.tan[...].astype(BF16)
    for k in range(4):
        out_copy(r, 0, k, owners.slot, owners.dst(k)).start()
    for k in range(4):
        curve = r.c_home[k].T[:64, 0:1]
        at = slice(64 * k, 64 * k + 64)
        r.grad[at, :] = curve * r.tan[at, :]
    for layer in (1, 0):
        dilation = r.dilations[layer]
        back = dot(r.grad[...].astype(BF16), r.point[layer], ((1,), (1,)))
        cells, halo, conv = r.gact.at[layer], r.ghalo.at[layer], r.conv.at[layer]
        cells[...] = (back * r.hslope[layer]).astype(BF16)
        finish = swap(2 + layer, cells, halo)
        act = dot(cells[...], conv[1], ((1,), (1,)))
        pick, pick_low, pick_high = pickers(dilation, rows)
        windows = dot(pick, cells[...], ((1,), (0,))).astype(BF16)
        act = act + dot(windows[:rows], conv[2], ((1,), (1,)))
        act = act + dot(windows[rows:], conv[0], ((1,), (1,)))
        r.grad[...] += r.slope[layer] * act
        finish()
        for n, tap, pick, at in ((0, 2, pick_low, 0), (1, 0, pick_high, rows - DMAX)):
            window = dot(pick, halo[n], ((1,), (0,))).astype(BF16)
            at = slice(at, at + DMAX)
            r.grad[at, :] += r.slope[layer, at, :] * dot(window, conv[tap], ((1,), (1,)))
    final = r.grad[...].astype(BF16)

    def send(t, carry):
        i = (j + 1 + t) % 8
        part = r.w_out[pl.ds(pl.multiple_of(i * VAL, 32), VAL), :]
        ga = dot(final, part, ((1,), (1,))).astype(BF16)

        @pl.when(t < 7)
        def _():
            r.ga_buf[i] = ga
            remote(r.ga_buf.at[i], r.item.at[j], r.g_send.at[i], r.g_recv.at[j], member(ctx, head, i)).start()

        @pl.when(t == 7)
        def _():
            r.item[j] = ga

        return carry

    lax.fori_loop(0, 8, send, 0)


def out_copy(r, n, k, slot, target):
    out = (r.out_t, r.out_c)[n]
    return remote(
        r.out_buf.at[n, pl.ds(64 * k, 64)], out.at[slot], r.o_send.at[n, k], r.o_recv.at[n, slot], target
    )


def back(r):
    ctx, head = me()
    j = chunk_of(ctx, head)
    owners, rows, line, column = owner_stream(), rows_stream(), line_stream(), column_stream()
    length = 8 * BLOCK
    r.q[...] = r.qt[:, KEY:]
    r.acc[...] = jnp.zeros(r.acc.shape, F32)
    for c in range(8):
        at = slice(c * BLOCK, (c + 1) * BLOCK)
        r.kT[:, at] = (r.kt[at, :].astype(F32).T[:KEY] * SCALE).astype(BF16)

    def ga_end(t, carry):
        i = (j + 1 + t) % 8
        remote(r.ga_buf.at[i], r.item.at[i], r.g_send.at[i], r.g_recv.at[i], member(ctx, head, i)).wait()
        return carry

    lax.fori_loop(0, 7, ga_end, 0)
    for c in range(8):
        at = slice(c * BLOCK, (c + 1) * BLOCK)
        prod = r.item[c].astype(F32) * r.att[at, :VAL]
        prod = jnp.concatenate([prod, jnp.zeros((BLOCK, 128 - VAL), F32)], axis=1)
        r.delta[:, at] = jnp.broadcast_to(jnp.sum(prod.T, axis=0, keepdims=True), (8, BLOCK))

    def packed(a):
        return jnp.concatenate([a[: BLOCK // 2], a[BLOCK // 2 :]], axis=1)

    def deliver(buf, ref, send, recv, i, t, value):
        @pl.when(t < 7)
        def _():
            buf[i] = value
            remote(buf.at[i], ref.at[j], send.at[i], recv.at[j], member(ctx, head, i)).start()

        @pl.when(t == 7)
        def _():
            ref[j] = value

    def block(t, carry):
        i = (j + 1 + t) % 8
        at = pl.ds(pl.multiple_of(i * BLOCK, BLOCK), BLOCK)
        g = r.item[...].reshape(length, VAL)
        s = dot(r.kt[at, :KEY], r.q[...], ((1,), (1,)))
        w = jnp.exp(s - r.lse[0:1, :])
        dp = dot(r.v[at, :VAL], g, ((1,), (1,)))
        ds = (w * (dp - r.delta[0:1, :])).astype(BF16)
        dv = dot(w.astype(BF16), g, ((1,), (0,))).astype(BF16)
        deliver(r.dv_buf, r.dv, r.v_send, r.v_recv, i, t, dv)
        dk = packed(dot(ds, r.q[...], ((1,), (0,))))
        deliver(r.dk_buf, r.dk, r.k_send, r.k_recv, i, t, dk.astype(BF16))
        dkT = dk.T
        r.pairT[KEY:, at] = jnp.concatenate([dkT[:KEY], dkT[KEY:]], axis=1).astype(BF16)
        r.acc[...] += dot(r.kT[:, at], ds, ((1,), (0,)))
        return carry

    lax.fori_loop(0, 8, block, 0)

    def dq_out(t, carry):
        i = (j + 1 + t) % 8
        at = pl.ds(pl.multiple_of(i * BLOCK, BLOCK), BLOCK)
        part = r.acc[:, at]
        dq = jnp.concatenate([part[:, : BLOCK // 2], part[:, BLOCK // 2 :]], axis=0).T.astype(BF16)
        deliver(r.dq_buf, r.dq, r.q_send, r.q_recv, i, t, dq)
        return carry

    lax.fori_loop(0, 8, dq_out, 0)
    r.pairT[:KEY, :] = r.acc[...].astype(BF16)
    part = dot(r.pairT[...], r.normed[...].reshape(length, -1), ((1,), (0,)))
    part = part.T
    size = part.shape[0] // 32
    for m in range(8):
        for i in range(4):
            n = 4 * m + i
            r.part_buf[i, m] = part[n * size : (n + 1) * size]
    r.part[line.own] = r.part_buf[line.own]

    def line_copy(d, slot):
        i = (line.own + d) % 4
        return remote(
            r.part_buf.at[i], r.part.at[i if slot is None else slot], r.e_send.at[i], r.e_recv.at[i if slot is None else slot],
            line.dst(i),
        )

    def column_copy(d, slot):
        m = (column.own + d) % 8
        return remote(
            r.half_buf.at[m], r.half.at[m if slot is None else slot], r.f_send.at[m], r.f_recv.at[m if slot is None else slot],
            column.dst(m),
        )

    for d in range(1, 4):
        line_copy(d, line.own).start()

    def early_end(t, carry):
        i = (j + 1 + t) % 8
        to = member(ctx, head, i)
        remote(r.dv_buf.at[i], r.dv.at[i], r.v_send.at[i], r.v_recv.at[i], to).wait()
        remote(r.dk_buf.at[i], r.dk.at[i], r.k_send.at[i], r.k_recv.at[i], to).wait()
        return carry

    lax.fori_loop(0, 7, early_end, 0)
    inputs = r.home[...].reshape(BLOCK, -1).astype(F32)
    count, features = inputs.shape

    def unpacked(a, b):
        top = jnp.concatenate([a[:, :KEY], b[:, :KEY]], axis=1)
        return jnp.concatenate([top, jnp.concatenate([a[:, KEY:], b[:, KEY:]], axis=1)], axis=0)

    acc = jnp.zeros((count, features), F32)
    for h in range(HEADS):
        acc = acc + dot(r.dv[h], r.wv[:, h * VAL : (h + 1) * VAL], ((1,), (1,)))
    for h in range(0, HEADS, 2):
        acc = acc + dot(unpacked(r.dk[h], r.dk[h + 1]), r.wk[:, h * KEY : (h + 2) * KEY], ((1,), (1,)))

    def late_end(t, carry):
        i = (j + 1 + t) % 8
        remote(r.dq_buf.at[i], r.dq.at[i], r.q_send.at[i], r.q_recv.at[i], member(ctx, head, i)).wait()
        return carry

    lax.fori_loop(0, 7, late_end, 0)
    for h in range(0, HEADS, 2):
        acc = acc + dot(unpacked(r.dq[h], r.dq[h + 1]), r.wq[:, h * KEY : (h + 2) * KEY], ((1,), (1,)))
    for d in range(1, 4):
        line_copy(d, None).wait()
    r.half_buf[...] = jnp.sum(r.part[...], axis=0)
    for d in range(1, 8):
        column_copy(d, column.own).start()
    r.half[column.own] = r.half_buf[column.own]
    gain = r.gain[...].reshape(1, -1)
    for k in range(4):
        at = slice(64 * k, 64 * k + 64)
        part_in = inputs[at]
        gained = acc[at] * gain
        spread = jnp.sqrt(jnp.mean(part_in * part_in, axis=-1, keepdims=True) + 1e-06)
        along = jnp.sum(gained * part_in, axis=-1, keepdims=True)
        r.out_buf[1, at, :] = (
            r.grad[at, :] + gained * (1.0 / spread) - part_in * (along / (features * spread * spread * spread))
        ).astype(BF16)
        out_copy(r, 1, k, owners.slot, owners.dst(k)).start()
    for d in range(1, 8):
        column_copy(d, None).wait()
    summed = jnp.sum(r.half[...], axis=0) * (1.0 / (32.0 * 2048.0))
    for k in range(8):
        r.rows[k, 0:3, :] = summed[3 * k : 3 * k + 3, :]
        r.rows[k, 3:8, :] = jnp.zeros((5, 2 * KEY), F32)
    for k in range(8):
        remote(r.rows.at[k], r.got.at[rows.slot], r.r_send.at[k], r.r_recv.at[rows.slot], rows.dst(k)).start()
    for k in range(8):
        remote(r.rows.at[k], r.got.at[k], r.r_send.at[k], r.r_recv.at[k], rows.dst(k)).wait()
    for k in range(8):
        r.gvq[:, k * KEY : (k + 1) * KEY] = r.got[k, 0:3, :KEY]
        r.gvk[:, k * KEY : (k + 1) * KEY] = r.got[k, 0:3, KEY:]
    for n in range(2):
        for k in range(4):
            out_copy(r, n, k, k, owners.dst(k)).wait()


WEIGHTS = ("tq", "wq", "wk", "tk", "wv", "w_out", "conv", "point")


def fetch(r, name):
    n = WEIGHTS.index(name)
    return pltpu.make_async_copy(getattr(r, name + "_hbm"), getattr(r, name), r.w_sem.at[n])


def whole_kernel(names, *refs):
    r = Refs(names, refs)
    barrier = pltpu.get_barrier_semaphore()
    greet_all(r, barrier)
    for name in WEIGHTS[:5]:
        fetch(r, name).start()
    pl.semaphore_wait(barrier, 33)
    front(r)
    attend_forward(r)
    conv_chain(r)
    back(r)


def run(inputs, collective_id):
    by_name = {name: array for name, array, _ in inputs}
    features = by_name["x"].shape[2]
    width = by_name["conv_hbm"].shape[3]
    length = 8 * BLOCK
    rows = BLOCK
    vmem, dma = pltpu.VMEM, pltpu.SemaphoreType.DMA
    scratch = {name: vmem(by_name[name + "_hbm"].shape, BF16) for name in WEIGHTS}
    scratch.update(
        w_sem=dma((len(WEIGHTS),)),
        home=vmem((4, 64, features), BF16),
        c_buf=vmem((4, 8, 128), F32),
        c_home=vmem((4, 8, 128), F32),
        joined=vmem((features, 384), BF16),
        normed=vmem((8, rows, features), BF16),
        qt=vmem((length, 128), BF16),
        kt=vmem((length, 128), BF16),
        v=vmem((length, 128), BF16),
        att_buf=vmem((8, 2, rows, VAL), BF16),
        attended=vmem((8, 2, rows, VAL), BF16),
        att=vmem((length, 128), F32),
        lse=vmem((8, length), F32),
        mixed=vmem((rows, features), F32),
        tan=vmem((rows, features), F32),
        grad=vmem((rows, features), F32),
        slope=vmem((2, rows, features), F32),
        hslope=vmem((2, rows, width), F32),
        act=vmem((2, 2, rows, features), BF16),
        inner=vmem((2, rows, width), F32),
        halo=vmem((2, 2, 2, DMAX, features), BF16),
        gact=vmem((2, rows, width), BF16),
        ghalo=vmem((2, 2, DMAX, width), BF16),
        out_buf=vmem((2, rows, features), BF16),
        ga_buf=vmem((8, rows, VAL), BF16),
        item=vmem((8, rows, VAL), BF16),
        q=vmem((length, KEY), BF16),
        kT=vmem((KEY, length), BF16),
        delta=vmem((8, length), F32),
        acc=vmem((KEY, length), F32),
        pairT=vmem((2 * KEY, length), BF16),
        dv_buf=vmem((8, rows, VAL), BF16),
        dv=vmem((8, rows, VAL), BF16),
        dk_buf=vmem((8, rows // 2, 2 * KEY), BF16),
        dk=vmem((8, rows // 2, 2 * KEY), BF16),
        dq_buf=vmem((8, rows // 2, 2 * KEY), BF16),
        dq=vmem((8, rows // 2, 2 * KEY), BF16),
        part_buf=vmem((4, 8, features // 32, 2 * KEY), F32),
        part=vmem((4, 8, features // 32, 2 * KEY), F32),
        half_buf=vmem((8, features // 32, 2 * KEY), F32),
        half=vmem((8, features // 32, 2 * KEY), F32),
        rows=vmem((8, 8, 2 * KEY), F32),
        got=vmem((8, 8, 2 * KEY), F32),
    )
    for name, shape in (
        ("x", (2, 4)),
        ("c", (4,)),
        ("n", (8, 8)),
        ("a", (8,)),
        ("h", (8,)),
        ("o", (2, 4)),
        ("g", (8,)),
        ("v", (8,)),
        ("k", (8,)),
        ("q", (8,)),
        ("e", (4,)),
        ("f", (8,)),
        ("r", (8,)),
    ):
        scratch[name + "_send"] = dma(shape + (3,)) if name == "n" else dma(shape)
        scratch[name + "_recv"] = dma(shape)
    outs = ("out_t", "out_c", "gvq", "gvk")
    names = [name for name, _, _ in inputs] + list(outs) + list(scratch)
    return pl.pallas_call(
        functools.partial(whole_kernel, names),
        out_shape=[
            jax.ShapeDtypeStruct((4, 64, features), BF16),
            jax.ShapeDtypeStruct((4, 64, features), BF16),
            jax.ShapeDtypeStruct((3, HEADS * KEY), F32),
            jax.ShapeDtypeStruct((3, HEADS * KEY), F32),
        ],
        in_specs=[pl.BlockSpec(memory_space=space) for _, _, space in inputs],
        out_specs=[pl.BlockSpec(memory_space=space) for space in (pl.ANY, pl.ANY, vmem, vmem)],
        scratch_shapes=list(scratch.values()),
        compiler_params=pltpu.CompilerParams(
            collective_id=collective_id, has_side_effects=True, vmem_limit_bytes=VMEM_LIMIT
        ),
    )(*[array for _, array, _ in inputs])


def deliver_kernel(*refs):
    count = len(refs) // 2
    for n in range(count):
        refs[count + n][...] = refs[n][...]


def deliver_all(arrays):
    return pl.pallas_call(
        deliver_kernel,
        out_shape=[jax.ShapeDtypeStruct(a.shape, a.dtype) for a in arrays],
        in_specs=[pl.BlockSpec(memory_space=pltpu.VMEM)] * len(arrays),
        out_specs=[pl.BlockSpec(memory_space=pltpu.VMEM)] * len(arrays),
    )(*arrays)


def per_device(
    window_input,
    norm_gain,
    w_query,
    w_key,
    w_value,
    w_out,
    conv_weight,
    point_weight,
    dilations,
    tangent_query,
    tangent_key,
    curvature,
):
    outs = run(
        (
            ("dilations", dilations, pltpu.SMEM),
            ("x", window_input, pl.ANY),
            ("curvature", curvature, pltpu.VMEM),
            ("gain", norm_gain, pltpu.VMEM),
            ("tq_hbm", tangent_query, pl.ANY),
            ("wq_hbm", w_query, pl.ANY),
            ("wk_hbm", w_key, pl.ANY),
            ("tk_hbm", tangent_key, pl.ANY),
            ("wv_hbm", w_value, pl.ANY),
            ("w_out_hbm", w_out, pl.ANY),
            ("conv_hbm", conv_weight, pl.ANY),
            ("point_hbm", point_weight, pl.ANY),
        ),
        0,
    )
    return tuple(deliver_all(outs))


def solution(mesh):
    in_specs = (P("head", "ctx", None),) + (P(),) * 10 + (P("head", "ctx"),)
    out_specs = (
        P("head", "ctx", None),
        P("head", "ctx", None),
        P(("ctx", "head"), None),
        P(("ctx", "head"), None),
    )
    return jax.shard_map(per_device, mesh=mesh, in_specs=in_specs, out_specs=out_specs, check_vma=False)
```
